256 devices in a mesh: seq: 32 (over z, x_hi, core), head: 8 (over x_lo, y).
Axes of the slice: x: 4 (x_hi: 2, x_lo: 2; x = x_hi * 2 + x_lo), y: 4, z: 8, core: 2. Of those that a mesh axis runs over, the one named last changes fastest.
Arguments:
- queries: bfloat16 [4, 65536, 1024], P(None, 'seq', 'head'), may hold values from -6 to 6
- keys_values: bfloat16 [4, 65536, 2, 1024], P(None, 'seq', None, 'head'), may hold values from -720 to 720
- norm_gain: float32 [1024], P('head'), may hold values from 0.1 to 1.9
Outputs:
- normalized: bfloat16 [4, 65536, 1024], P(None, 'seq', 'head')
The draws below stay inside these ranges and needn't reach their ends.
All inputs are finite; a program needn't handle non-finite values.
Results may differ from the reference program's by a relative error of at most 0.005.
Values may be sent and summed in bfloat16 or wider, within the bound.
A program may use at most 64 MiB of HBM per device.

```python
import math
from functools import reduce
import jax
import jax.numpy as jnp
from jax import lax

HD = 128
P_SIZE = 16
SEQS = 4
HEADS = 8
D = 1024
SEQLEN = 65536


def draw_queries(key, part):
    key = jax.random.fold_in(key, 11)
    result = jnp.clip(jax.random.normal(key, (SEQS, SEQLEN, D), jnp.float32), -4.5, 4.5)
    return result.astype(jnp.bfloat16)


def draw_keys_values(key, part):
    key = jax.random.fold_in(key, 23)
    key_part, rough_key, coarse_key, coarser_key = jax.random.split(key, 4)
    key_array = jnp.clip(jax.random.normal(key_part, (SEQS, SEQLEN, D), jnp.float32), -4.5, 4.5)
    rough_part = jnp.clip(jax.random.normal(rough_key, (SEQS, SEQLEN, D), jnp.float32), -4.0, 4.0)
    head_base = 3.0
    coarse_two = jnp.clip(jax.random.normal(coarse_key, (SEQS, SEQLEN // (P_SIZE * P_SIZE), D), jnp.float32), -2.0, 2.0)
    coarse_three = jnp.clip(jax.random.normal(coarser_key, (SEQS, SEQLEN // P_SIZE ** 3, D), jnp.float32), -2.0, 2.0)
    smooth_part = jnp.repeat(coarse_two, P_SIZE * P_SIZE, axis=1) + jnp.repeat(coarse_three, P_SIZE ** 3, axis=1)
    head_index = (jnp.arange(D) // HD).astype(jnp.float32)
    head_scale = head_base ** (head_index / max(HEADS - 1, 1))
    value_array = (rough_part + smooth_part) * head_scale[None, None, :]
    return jnp.stack([key_array, value_array], axis=2).astype(jnp.bfloat16)


def setup_inputs(seed: int = 0) -> dict:
    arg_keys = jax.random.split(jax.random.key(seed), 4)
    return {
        "queries": draw_queries(jax.random.fold_in(arg_keys[3], 71), 0),
        "keys_values": draw_keys_values(jax.random.fold_in(arg_keys[3], 71), 0),
        "norm_gain": jnp.clip(1.0 + 0.18 * jax.random.normal(arg_keys[2], (D,), jnp.float32), 0.1, 1.9),
    }


def pool(source):
    batch_size, cells = (source.shape[0], source.shape[1])
    grouped = source.reshape(batch_size, cells // P_SIZE, P_SIZE, source.shape[2], source.shape[3]).astype(jnp.float32)
    return (lax.optimization_barrier(jnp.sum(grouped, axis=2)) / P_SIZE).astype(jnp.bfloat16)

def attend(query_block, key_groups, query_pos, group_pos, seq_length):
    block_len = P_SIZE * P_SIZE
    margin_len = block_len // 2
    cube_len = P_SIZE ** 3
    block_start = query_pos // block_len * block_len
    near_lo = block_start - margin_len
    near_hi = block_start + block_len + margin_len
    first_lo = block_start - 2 * block_len
    first_hi = block_start + 3 * block_len
    second_lo = first_lo // cube_len * cube_len - cube_len
    second_hi = -(-first_hi // cube_len) * cube_len + cube_len

    def inside(positions, lower, upper):
        return (positions[None, :] >= lower[:, None]) & (positions[None, :] < upper[:, None])

    def present(positions):
        return ((positions >= 0) & (positions < seq_length))[None, :]
    key_masks = [inside(group_pos[0], near_lo, near_hi) & present(group_pos[0]), inside(group_pos[1], first_lo, first_hi) & ~inside(group_pos[1], near_lo, near_hi) & present(group_pos[1]), inside(group_pos[2], second_lo, second_hi) & ~inside(group_pos[2], first_lo, first_hi) & present(group_pos[2]), ~inside(group_pos[3], second_lo, second_hi) & present(group_pos[3])]
    head_dim = query_block.shape[-1]
    query_wide = query_block.astype(jnp.float32)
    scores = []
    for level_num in range(4):
        keys_wide = key_groups[level_num][:, :, 0].astype(jnp.float32)
        raw_score = jnp.einsum('sqhe,skhe->shqk', query_wide, keys_wide)
        shifted = raw_score / math.sqrt(head_dim) + level_num * math.log(P_SIZE) / 2
        scores.append(jnp.where(key_masks[level_num][None, None], shifted, -jnp.inf))
    row_max = reduce(jnp.maximum, [lax.optimization_barrier(jnp.max(score, axis=-1)) for score in scores])
    totals = []
    products = []
    for level_num in range(4):
        weight = jnp.exp(scores[level_num] - row_max[..., None])
        totals.append(lax.optimization_barrier(jnp.sum(weight, axis=-1)))
        rounded = lax.optimization_barrier(weight.astype(jnp.bfloat16))
        values_wide = key_groups[level_num][:, :, 1].astype(jnp.float32)
        products.append(jnp.einsum('shqk,skhe->sqhe', rounded.astype(jnp.float32), values_wide))
    row_total = totals[0] + totals[1] + totals[2] + totals[3]
    weighted = products[0] + products[1] + products[2] + products[3]
    return (weighted / jnp.transpose(row_total, (0, 2, 1))[..., None]).astype(jnp.bfloat16)

def reference(queries, keys_values, norm_gain):
    batch_size, seq_length, full_width = queries.shape
    head_count = full_width // HD
    block_len = P_SIZE * P_SIZE
    margin_len = block_len // 2
    cube_len = P_SIZE ** 3
    level_one = pool(keys_values)
    level_two = pool(level_one)
    level_three = pool(level_two)

    def split_heads(source):
        return source.reshape(batch_size, source.shape[1], 2, head_count, HD)
    query_heads = queries.reshape(batch_size, seq_length, head_count, HD)
    near_pad = jnp.pad(split_heads(keys_values), ((0, 0), (margin_len, margin_len), (0, 0), (0, 0), (0, 0)))
    one_pad = jnp.pad(split_heads(level_one), ((0, 0), (2 * P_SIZE, 2 * P_SIZE), (0, 0), (0, 0), (0, 0)))
    two_heads = split_heads(level_two)
    three_heads = split_heads(level_three)
    two_pos = jnp.arange(seq_length // block_len, dtype=jnp.int32) * block_len
    three_pos = jnp.arange(seq_length // cube_len, dtype=jnp.int32) * cube_len

    def one_block(block_num):
        block_start = (block_num * block_len).astype(jnp.int32)
        query_block = lax.dynamic_slice_in_dim(query_heads, block_start, block_len, 1)
        near_keys = lax.dynamic_slice_in_dim(near_pad, block_start, block_len + 2 * margin_len, 1)
        near_pos = block_start - margin_len + jnp.arange(block_len + 2 * margin_len, dtype=jnp.int32)
        first_cell = (block_start // P_SIZE).astype(jnp.int32)
        first_keys = lax.dynamic_slice_in_dim(one_pad, first_cell, 5 * P_SIZE, 1)
        first_pos = block_start - 2 * block_len + jnp.arange(5 * P_SIZE, dtype=jnp.int32) * P_SIZE
        query_pos = block_start + jnp.arange(block_len, dtype=jnp.int32)
        return attend(query_block, [near_keys, first_keys, two_heads, three_heads], query_pos, [near_pos, first_pos, two_pos, three_pos], seq_length)
    blocks = lax.map(one_block, jnp.arange(seq_length // block_len, dtype=jnp.int32))
    attention = jnp.transpose(blocks, (1, 0, 2, 3, 4)).reshape(batch_size, seq_length, full_width)
    attention_wide = attention.astype(jnp.float32)
    square_sum = lax.optimization_barrier(jnp.sum(attention_wide * attention_wide, axis=-1))
    scale_row = 1.0 / jnp.sqrt(square_sum / full_width + 1e-06)
    return (attention_wide * scale_row[..., None] * norm_gain).astype(jnp.bfloat16)
```

```python
import functools
import math

import jax
import jax.numpy as jnp
from jax import lax
from jax.experimental import pallas as pl
from jax.experimental.pallas import tpu as pltpu
from jax.sharding import PartitionSpec as P

HD = 128
CELL = 16
BLK = 256
CUBE = 4096
MARGIN = 128
NEAR = 512
LOW = 24
EXTRA = 128
ROWS = 272
NEG = -1e30
EXP_SCALE = math.log2(math.e) / math.sqrt(HD)
LEVEL_STEP = 2.0 / EXP_SCALE
MESH = pl.DeviceIdType.MESH
F32 = jnp.float32
BF16 = jnp.bfloat16


def dot_nt(a, b):
    return lax.dot_general(a, b, (((1,), (1,)), ((), ())), preferred_element_type=F32)


def dot_nn(a, b):
    return lax.dot_general(a, b, (((1,), (0,)), ((), ())), preferred_element_type=F32)


def iota(shape, dim):
    return lax.broadcasted_iota(jnp.int32, shape, dim)


def split_matrix():
    row = iota((ROWS, BLK), 0)
    col = iota((ROWS, BLK), 1)
    keys = (row < MARGIN) & (col == 2 * row)
    values = (row >= MARGIN) & (row < BLK) & (col == 2 * (row - MARGIN) + 1)
    cell = row - BLK
    pooled = (row >= BLK) & (col // (2 * CELL) == cell % 8) & (col % 2 == cell // 8)
    return jnp.where(
        keys | values, 1.0, jnp.where(pooled, 1.0 / CELL, 0.0)
    ).astype(BF16)


def fmm_kernel(
    n_seq,
    n_head,
    q_hbm,
    kv_hbm,
    att_hbm,
    total_hbm,
    raw,
    q_buf,
    k_buf,
    v_buf,
    k1,
    v1,
    k23,
    v23,
    tok_recv,
    cells_send,
    cells_recv,
    pair,
    cube_recv,
    third_send,
    third,
    att,
    own_sum,
    sums,
    total,
    splitter,
    q_sem,
    kv_sem,
    out_sem,
    tok_ssem,
    tok_rsem,
    cells_ssem,
    cells_rsem,
    pair_ssem,
    pair_rsem,
    cube_ssem,
    cube_rsem,
    third_ssem,
    third_rsem,
    sum_ssem,
    sum_rsem,
):
    seqs, toks, _ = q_hbm.shape
    blocks = toks // BLK
    cells = toks // CELL
    cubes = n_seq // 2
    seq_len = n_seq * toks
    me = lax.axis_index("seq")
    head = lax.axis_index("head")
    core = me % 2
    chip = me // 2
    dev_start = me * toks
    has_low = me > 0
    has_high = me < n_seq - 1

    for s in range(seqs):
        pltpu.make_async_copy(kv_hbm.at[s], raw.at[s], kv_sem.at[s]).start()
    for s in range(seqs):
        pltpu.make_async_copy(q_hbm.at[s], q_buf.at[s], q_sem.at[s]).start()

    barrier = pltpu.get_barrier_semaphore()

    def greet(seq_id, head_id):
        pl.semaphore_signal(
            barrier, inc=1, device_id=(seq_id, head_id), device_id_type=MESH
        )

    greet(me + 1 - 2 * core, head)
    for k in range(1, cubes):
        greet((chip + k) % cubes * 2 + core, head)
    for k in range(1, n_head):
        greet(me, (head + k) % n_head)
    outer = me - 1 + 2 * core
    outer_there = (outer >= 0) & (outer < n_seq)

    @pl.when(outer_there)
    def _():
        greet(outer, head)

    splitter[...] = split_matrix()
    v_buf[:, :, HD:] = jnp.ones((seqs, toks + BLK, HD), BF16)
    spare = 16 - (cubes - 1)
    third[(cubes - 1) * 8 :, :] = jnp.zeros((spare * 8, HD), F32)
    k23[...] = jnp.zeros_like(k23)
    v23[...] = jnp.zeros_like(v23)

    @pl.when(jnp.logical_not(has_low))
    def _():
        k_buf[:, :MARGIN, :] = jnp.zeros((seqs, MARGIN, HD), BF16)
        v_buf[:, :MARGIN, :HD] = jnp.zeros((seqs, MARGIN, HD), BF16)
        k1[:, :32, :] = jnp.zeros((seqs, 32, HD), F32)
        v1[:, :32, :] = jnp.zeros((seqs, 32, HD), F32)

    @pl.when(jnp.logical_not(has_high))
    def _():
        k_buf[:, MARGIN + toks :, :] = jnp.zeros((seqs, MARGIN, HD), BF16)
        v_buf[:, MARGIN + toks :, :HD] = jnp.zeros((seqs, MARGIN, HD), BF16)
        k1[:, 32 + cells :, :] = jnp.zeros((seqs, 32, HD), F32)
        v1[:, 32 + cells :, :] = jnp.zeros((seqs, 32, HD), F32)

    pl.semaphore_wait(barrier, cubes + n_head - 1 + outer_there.astype(jnp.int32))

    def token_copy(side):
        rows = pl.ds(0, BLK) if side == 0 else pl.ds(2 * toks - BLK, BLK)
        return pltpu.make_async_remote_copy(
            src_ref=kv_hbm.at[:, rows, :],
            dst_ref=tok_recv.at[1 - side],
            send_sem=tok_ssem.at[side],
            recv_sem=tok_rsem.at[1 - side],
            device_id=(me - 1 if side == 0 else me + 1, head),
            device_id_type=MESH,
        )

    def cells_copy(side):
        return pltpu.make_async_remote_copy(
            src_ref=cells_send.at[side],
            dst_ref=cells_recv.at[1 - side],
            send_sem=cells_ssem.at[side],
            recv_sem=cells_rsem.at[1 - side],
            device_id=(me - 1 if side == 0 else me + 1, head),
            device_id_type=MESH,
        )

    there = (has_low, has_high)
    for side in range(2):

        @pl.when(there[side])
        def _(side=side):
            token_copy(side).start()

    def split_chunk(source, s, dst):
        parts = dot_nn(splitter[...], source)
        k_buf[s, pl.ds(dst, MARGIN), :] = parts[:MARGIN].astype(BF16)
        v_buf[s, pl.ds(dst, MARGIN), :HD] = parts[MARGIN:BLK].astype(BF16)
        return parts

    for s in range(seqs):
        pltpu.make_async_copy(kv_hbm.at[s], raw.at[s], kv_sem.at[s]).wait()

        def chunk(j, carry, s=s):
            start = pl.multiple_of(j * BLK, BLK)
            dst = pl.multiple_of(j * MARGIN + MARGIN, MARGIN)
            parts = split_chunk(raw[s, pl.ds(start, BLK), :], s, dst)
            at = pl.multiple_of(j * 8 + 32, 8)
            k1[s, pl.ds(at, 8), :] = parts[BLK : BLK + 8].astype(BF16).astype(F32)
            v1[s, pl.ds(at, 8), :] = parts[BLK + 8 :].astype(BF16).astype(F32)
            return carry

        lax.fori_loop(0, 2 * toks // BLK, chunk, 0, unroll=4)

    for side in range(2):
        at = 32 if side == 0 else cells
        for s in range(seqs):
            cells_send[side, s, :32, :] = k1[s, at : at + 32, :].astype(BF16)
            cells_send[side, s, 32:, :] = v1[s, at : at + 32, :].astype(BF16)

        @pl.when(there[side])
        def _(side=side):
            cells_copy(side).start()

    pool_row = iota((CELL, 2 * cells), 0)
    pool_col = iota((CELL, 2 * cells), 1)
    pool_two = jnp.where(pool_col // CELL == pool_row, 1.0 / CELL, 0.0).astype(BF16)
    for s in range(seqs):
        ones_kv = jnp.concatenate(
            [k1[s, 32 : 32 + cells, :], v1[s, 32 : 32 + cells, :]], axis=0
        ).astype(BF16)
        pair[core, s] = dot_nn(pool_two, ones_kv).astype(BF16)
    pair_copy = pltpu.make_async_remote_copy(
        src_ref=pair.at[core],
        dst_ref=pair.at[core],
        send_sem=pair_ssem,
        recv_sem=pair_rsem,
        device_id=(me + 1 - 2 * core, head),
        device_id_type=MESH,
    )
    pair_copy.start()
    pair_copy.wait()

    def cube_copy(slot):
        target = chip + 2 - core - slot
        return pltpu.make_async_remote_copy(
            src_ref=pair,
            dst_ref=cube_recv.at[slot],
            send_sem=cube_ssem.at[slot],
            recv_sem=cube_rsem.at[slot],
            device_id=(target * 2 + core, head),
            device_id_type=MESH,
        )

    def cube_goes(slot):
        target = chip + 2 - core - slot
        return (target >= 0) & (target < cubes) & (slot != 2 - core)

    def cube_comes(slot):
        source = chip - 2 + core + slot
        return (source >= 0) & (source < cubes) & (slot != 2 - core)

    for s in range(seqs):
        both = pair[0, s].astype(F32) + pair[1, s].astype(F32)
        for half in range(2):
            mean = jnp.sum(both[8 * half : 8 * half + 8], axis=0, keepdims=True) / CELL
            third_send[2 * s + half : 2 * s + half + 1, :] = mean.astype(BF16).astype(F32)

    def third_copy(k):
        return pltpu.make_async_remote_copy(
            src_ref=third_send,
            dst_ref=third.at[pl.ds((cubes - 1 - k) * 8, 8), :],
            send_sem=third_ssem.at[k],
            recv_sem=third_rsem.at[cubes - 1 - k],
            device_id=((chip + k) % cubes * 2 + core, head),
            device_id_type=MESH,
        )

    for k in range(1, cubes):
        third_copy(k).start()
    for slot in range(4):

        @pl.when(cube_goes(slot))
        def _(slot=slot):
            cube_copy(slot).start()

    for k in range(1, cubes):
        third_copy(k).wait_recv()
    for s in range(seqs):
        k23[s, 64:, :] = third[pl.ds(2 * s, 16, stride=8), :]
        v23[s, 64:, :] = third[pl.ds(2 * s + 1, 16, stride=8), :]
    for slot in range(4):
        for half in range(2):
            at = slot * 16 + half * 8

            @pl.when(slot == 2 - core)
            def _(half=half, at=at):
                for s in range(seqs):
                    tile = pair[half, s].astype(F32)
                    k23[s, at : at + 8, :] = tile[:8]
                    v23[s, at : at + 8, :] = tile[8:]

            @pl.when(cube_comes(slot))
            def _(slot=slot, half=half, at=at):
                if half == 0:
                    cube_copy(slot).wait_recv()
                for s in range(seqs):
                    tile = cube_recv[slot, half, s].astype(F32)
                    k23[s, at : at + 8, :] = tile[:8]
                    v23[s, at : at + 8, :] = tile[8:]

    lane = iota((1, EXTRA), 1)
    ones_row = jnp.ones((16, HD), BF16)
    ones_tile = jnp.ones((EXTRA, HD), BF16)

    def extra_bias(b):
        start = dev_start + b * BLK
        first_lo = start - 2 * BLK
        first_hi = start + 3 * BLK
        second_lo = (first_lo + CUBE) // CUBE * CUBE - 2 * CUBE
        second_hi = (first_hi + CUBE - 1) // CUBE * CUBE + CUBE
        one_pos = jnp.where(
            lane < LOW, first_lo + lane * CELL, start + 384 + (lane - LOW) * CELL
        )
        two_pos = ((chip - 2 + core) * 16 + lane - 2 * LOW) * BLK
        third_slot = lane - 112
        third_cube = (chip + 1 + third_slot) % cubes
        three_pos = third_cube * CUBE
        one_ok = (one_pos >= 0) & (one_pos < seq_len)
        two_ok = (
            (two_pos >= 0)
            & (two_pos < seq_len)
            & (two_pos >= second_lo)
            & (two_pos < second_hi)
            & ((two_pos < first_lo) | (two_pos >= first_hi))
        )
        three_ok = (third_slot < cubes - 1) & (
            (three_pos < second_lo) | (three_pos >= second_hi)
        )
        return jnp.where(
            lane < 2 * LOW,
            jnp.where(one_ok, LEVEL_STEP, NEG),
            jnp.where(
                lane < 112,
                jnp.where(two_ok, 2 * LEVEL_STEP, NEG),
                jnp.where(three_ok, 3 * LEVEL_STEP, NEG),
            ),
        )

    def near_bias(b):
        pos = dev_start + b * BLK - MARGIN + iota((1, NEAR), 1)
        return jnp.where((pos >= 0) & (pos < seq_len), 0.0, NEG)

    def attend(s, b, edge):
        at = pl.multiple_of(b * BLK, BLK)
        cell_at = pl.multiple_of(b * CELL, CELL)
        q = q_buf[s, pl.ds(at, BLK), :]
        near_k = k_buf[s, pl.ds(at, NEAR), :]
        near_v = v_buf[s, pl.ds(at, NEAR), :]

        def extras(one, rest):
            return jnp.concatenate(
                [
                    one[s, pl.ds(cell_at, LOW), :],
                    one[s, pl.ds(pl.multiple_of(cell_at + 56, 8), LOW), :],
                    rest[s],
                ],
                axis=0,
            ).astype(BF16)

        extra_k = extras(k1, k23)
        extra_v = jnp.concatenate([extras(v1, v23), ones_tile], axis=1)
        near_s = dot_nt(q, near_k)
        if edge:
            near_s = near_s + near_bias(b)
        extra_s = dot_nt(q, extra_k) + extra_bias(b)
        top = jnp.maximum(
            jnp.max(near_s, axis=1, keepdims=True),
            jnp.max(extra_s, axis=1, keepdims=True),
        )
        near_w = jnp.exp2((near_s - top) * EXP_SCALE).astype(BF16)
        extra_w = jnp.exp2((extra_s - top) * EXP_SCALE).astype(BF16)
        out = dot_nn(near_w, near_v) + dot_nn(extra_w, extra_v)
        result = (out[:, :HD] / out[:, HD:]).astype(BF16)
        att[s, pl.ds(at, BLK), :] = result
        wide = result.astype(F32)
        square = dot_nt(ones_row, (wide * wide).astype(BF16))
        own_sum[b, 2 * s : 2 * s + 1, :] = square[:1, :HD]
        own_sum[b, 2 * s + 1 : 2 * s + 2, :] = square[:1, HD:]

    def att_copy(b):
        rows = pl.ds(pl.multiple_of(b * BLK, BLK), BLK)
        return pltpu.make_async_copy(
            att.at[:, rows, :], att_hbm.at[:, rows, :], out_sem.at[b]
        )

    def sum_copy(b, k):
        return pltpu.make_async_remote_copy(
            src_ref=own_sum.at[b],
            dst_ref=sums.at[b, n_head - 1 - k],
            send_sem=sum_ssem.at[b, k],
            recv_sem=sum_rsem.at[b, n_head - 1 - k],
            device_id=(me, (head + k) % n_head),
            device_id_type=MESH,
        )

    def run_block(b, edge):
        for s in range(seqs):
            attend(s, b, edge)
        att_copy(b).start()
        for k in range(1, n_head):
            sum_copy(b, k).start()

    for s in range(seqs):
        pltpu.make_async_copy(q_hbm.at[s], q_buf.at[s], q_sem.at[s]).wait()

    def inner(b, carry):
        run_block(b, False)
        return carry

    lax.fori_loop(2, blocks - 2, inner, 0)

    for side in range(2):

        @pl.when(there[side])
        def _(side=side):
            cells_copy(1 - side).wait_recv()
            at = 0 if side == 0 else 32 + cells
            for s in range(seqs):
                k1[s, at : at + 32, :] = cells_recv[side, s, :32, :].astype(F32)
                v1[s, at : at + 32, :] = cells_recv[side, s, 32:, :].astype(F32)

    def second_inner(i, carry):
        run_block(1 + i * (blocks - 3), False)
        return carry

    lax.fori_loop(0, 2, second_inner, 0)

    for side in range(2):

        @pl.when(there[side])
        def _(side=side):
            token_copy(1 - side).wait_recv()
            at = 0 if side == 0 else MARGIN + toks
            for s in range(seqs):
                split_chunk(tok_recv[side, s], s, at)

    def outermost(i, carry):
        run_block(i * (blocks - 1), True)
        return carry

    lax.fori_loop(0, 2, outermost, 0)

    def add_up(b, carry):
        acc = own_sum[b]
        for k in range(1, n_head):
            sum_copy(b, k).wait_recv()
        for k in range(n_head - 1):
            acc = acc + sums[b, k]
        total[b] = acc
        return carry

    lax.fori_loop(0, blocks, add_up, 0)
    total_copy = pltpu.make_async_copy(total, total_hbm, out_sem.at[blocks])
    total_copy.start()

    def drain(b, carry):
        att_copy(b).wait()
        for k in range(1, n_head):
            sum_copy(b, k).wait_send()
        return carry

    lax.fori_loop(0, blocks, drain, 0)
    for side in range(2):

        @pl.when(there[side])
        def _(side=side):
            token_copy(side).wait_send()
            cells_copy(side).wait_send()

    for slot in range(4):

        @pl.when(cube_goes(slot))
        def _(slot=slot):
            cube_copy(slot).wait_send()

    for k in range(1, cubes):
        third_copy(k).wait_send()
    total_copy.wait()


def attention(queries, pairs, n_seq, n_head):
    seqs, toks, _ = queries.shape
    blocks = toks // BLK
    cells = toks // CELL
    cubes = n_seq // 2
    assert toks == CUBE // 2 and cubes <= 16 and 2 * seqs <= 8
    vmem = pltpu.VMEM
    dma = pltpu.SemaphoreType.DMA
    hbm = pl.BlockSpec(memory_space=pl.ANY)
    return pl.pallas_call(
        functools.partial(fmm_kernel, n_seq, n_head),
        out_shape=(
            jax.ShapeDtypeStruct((seqs, toks, HD), BF16),
            jax.ShapeDtypeStruct((blocks, 8, HD), F32),
        ),
        in_specs=[hbm, hbm],
        out_specs=(hbm, hbm),
        scratch_shapes=[
            vmem((seqs, 2 * toks, HD), BF16),
            vmem((seqs, toks, HD), BF16),
            vmem((seqs, toks + BLK, HD), BF16),
            vmem((seqs, toks + BLK, 2 * HD), BF16),
            vmem((seqs, cells + 64, HD), F32),
            vmem((seqs, cells + 64, HD), F32),
            vmem((seqs, 80, HD), F32),
            vmem((seqs, 80, HD), F32),
            vmem((2, seqs, BLK, HD), BF16),
            vmem((2, seqs, 64, HD), BF16),
            vmem((2, seqs, 64, HD), BF16),
            vmem((2, seqs, CELL, HD), BF16),
            vmem((4, 2, seqs, CELL, HD), BF16),
            vmem((8, HD), F32),
            vmem((16 * 8, HD), F32),
            vmem((seqs, toks, HD), BF16),
            vmem((blocks, 8, HD), F32),
            vmem((blocks, n_head - 1, 8, HD), F32),
            vmem((blocks, 8, HD), F32),
            vmem((ROWS, BLK), BF16),
            dma((seqs,)),
            dma((seqs,)),
            dma((blocks + 1,)),
            dma((2,)),
            dma((2,)),
            dma((2,)),
            dma((2,)),
            dma(()),
            dma(()),
            dma((4,)),
            dma((4,)),
            dma((16,)),
            dma((16,)),
            dma((blocks, n_head)),
            dma((blocks, n_head)),
        ],
        compiler_params=pltpu.CompilerParams(
            collective_id=0, has_side_effects=True, vmem_limit_bytes=56 * 2**20
        ),
        cost_estimate=pl.CostEstimate(
            flops=4 * seqs * toks * 640 * HD,
            bytes_accessed=8 * seqs * toks * HD,
            transcendentals=seqs * toks * 640,
        ),
    )(queries, pairs)


def on_device(n_seq, n_head, queries, keys_values, norm_gain):
    seqs, toks, width = queries.shape
    pairs = keys_values.reshape(seqs, 2 * toks, width)
    att, total = attention(queries, pairs, n_seq, n_head)
    blocks = toks // BLK
    square_sum = total[:, : 2 * seqs].reshape(blocks, seqs, BLK)
    square_sum = jnp.transpose(square_sum, (1, 0, 2)).reshape(seqs, toks)
    scale_row = 1.0 / jnp.sqrt(square_sum / (HD * n_head) + 1e-06)
    return (att.astype(F32) * scale_row[..., None] * norm_gain).astype(BF16)


def solution(mesh):
    n_seq, n_head = mesh.shape["seq"], mesh.shape["head"]
    in_specs = (P(None, "seq", "head"), P(None, "seq", None, "head"), P("head"))
    return jax.shard_map(
        functools.partial(on_device, n_seq, n_head),
        mesh=mesh,
        in_specs=in_specs,
        out_specs=P(None, "seq", "head"),
        check_vma=False,
    )
```

```python
import functools
import math

import jax
import jax.numpy as jnp
from jax import lax
from jax.experimental import pallas as pl
from jax.experimental.pallas import tpu as pltpu
from jax.sharding import PartitionSpec as P

HD = 128
CELL = 16
BLK = 256
CUBE = 4096
MARGIN = 128
NEAR = 512
LOW = 24
EXTRA = 128
TWO_PASS = (6, 3)
EARLY = 2
NEG = -1e30
EXP_SCALE = math.log2(math.e) / math.sqrt(HD)
LEVEL_STEP = 2.0 / EXP_SCALE
MESH = pl.DeviceIdType.MESH
F32 = jnp.float32
BF16 = jnp.bfloat16


def dot_nt(a, b):
    return lax.dot_general(a, b, (((1,), (1,)), ((), ())), preferred_element_type=F32)


def dot_nn(a, b):
    return lax.dot_general(a, b, (((1,), (0,)), ((), ())), preferred_element_type=F32)


def iota(shape, dim):
    return lax.broadcasted_iota(jnp.int32, shape, dim)


def split_matrix():
    row = iota((BLK, BLK), 0)
    col = iota((BLK, BLK), 1)
    return (col == 2 * (row % MARGIN) + row // MARGIN).astype(BF16)


def pool_matrix():
    row = iota((CELL, BLK), 0)
    col = iota((CELL, BLK), 1)
    picked = (col // (2 * CELL) == row % 8) & (col % 2 == row // 8)
    return jnp.where(picked, 1.0 / CELL, 0.0).astype(BF16)


def fmm_kernel(
    n_seq,
    n_head,
    q_hbm,
    kv_hbm,
    gain_ref,
    att,
    raw,
    q_buf,
    k_buf,
    v_buf,
    k1,
    v1,
    k23,
    v23,
    tok_recv,
    cells_send,
    cells_recv,
    pair,
    cube_recv,
    third_send,
    third,
    near_out,
    near_top,
    own_sum,
    sums,
    splitter,
    q_sem,
    kv_sem,
    tok_ssem,
    tok_rsem,
    cells_ssem,
    cells_rsem,
    pair_ssem,
    pair_rsem,
    cube_ssem,
    cube_rsem,
    third_ssem,
    third_rsem,
    sum_ssem,
    sum_rsem,
):
    seqs, toks, _ = q_hbm.shape
    blocks = toks // BLK
    cells = toks // CELL
    cubes = n_seq // 2
    seq_len = n_seq * toks
    me = lax.axis_index("seq")
    head = lax.axis_index("head")
    core = me % 2
    chip = me // 2
    dev_start = me * toks
    parts = ((0, blocks - 2), (blocks - 2, 2))
    first_half = me < n_seq // 2
    early = jnp.where(first_half, EARLY, 0)
    two_pass = jnp.where(first_half, *TWO_PASS)
    has_low = me > 0
    has_high = me < n_seq - 1

    for s in range(seqs):
        pltpu.make_async_copy(kv_hbm.at[s], raw.at[s], kv_sem.at[s]).start()
    for s in range(seqs):
        pltpu.make_async_copy(q_hbm.at[s], q_buf.at[s], q_sem.at[s]).start()

    barrier = pltpu.get_barrier_semaphore()

    def greet(seq_id, head_id):
        pl.semaphore_signal(
            barrier, inc=1, device_id=(seq_id, head_id), device_id_type=MESH
        )

    greet(me + 1 - 2 * core, head)
    for k in range(1, cubes):
        greet((chip + k) % cubes * 2 + core, head)
    for k in range(1, n_head):
        greet(me, (head + k) % n_head)
    outer = me - 1 + 2 * core
    outer_there = (outer >= 0) & (outer < n_seq)

    @pl.when(outer_there)
    def _():
        greet(outer, head)

    splitter[...] = split_matrix()
    v_buf[:, :, HD:] = jnp.ones((seqs, toks + BLK, HD), BF16)
    spare = 16 - (cubes - 1)
    third[(cubes - 1) * 8 :, :] = jnp.zeros((spare * 8, HD), F32)
    k23[...] = jnp.zeros_like(k23)
    v23[...] = jnp.zeros_like(v23)

    @pl.when(jnp.logical_not(has_low))
    def _():
        k_buf[:, :MARGIN, :] = jnp.zeros((seqs, MARGIN, HD), BF16)
        v_buf[:, :MARGIN, :HD] = jnp.zeros((seqs, MARGIN, HD), BF16)
        k1[:, :32, :] = jnp.zeros((seqs, 32, HD), F32)
        v1[:, :32, :] = jnp.zeros((seqs, 32, HD), F32)

    @pl.when(jnp.logical_not(has_high))
    def _():
        k_buf[:, MARGIN + toks :, :] = jnp.zeros((seqs, MARGIN, HD), BF16)
        v_buf[:, MARGIN + toks :, :HD] = jnp.zeros((seqs, MARGIN, HD), BF16)
        k1[:, 32 + cells :, :] = jnp.zeros((seqs, 32, HD), F32)
        v1[:, 32 + cells :, :] = jnp.zeros((seqs, 32, HD), F32)


    def token_copy(side):
        rows = pl.ds(0, BLK) if side == 0 else pl.ds(2 * toks - BLK, BLK)
        return pltpu.make_async_remote_copy(
            src_ref=kv_hbm.at[:, rows, :],
            dst_ref=tok_recv.at[1 - side],
            send_sem=tok_ssem.at[side],
            recv_sem=tok_rsem.at[1 - side],
            device_id=(me - 1 if side == 0 else me + 1, head),
            device_id_type=MESH,
        )

    def cells_copy(side):
        return pltpu.make_async_remote_copy(
            src_ref=cells_send.at[side],
            dst_ref=cells_recv.at[1 - side],
            send_sem=cells_ssem.at[side],
            recv_sem=cells_rsem.at[1 - side],
            device_id=(me - 1 if side == 0 else me + 1, head),
            device_id_type=MESH,
        )

    there = (has_low, has_high)
    pooler = pool_matrix()
    for s in range(seqs):
        pltpu.make_async_copy(kv_hbm.at[s], raw.at[s], kv_sem.at[s]).wait()

        def pool_chunk(j, carry, s=s):
            start = pl.multiple_of(j * BLK, BLK)
            cell = dot_nn(pooler, raw[s, pl.ds(start, BLK), :])
            at = pl.multiple_of(j * 8 + 32, 8)
            k1[s, pl.ds(at, 8), :] = cell[:8].astype(BF16).astype(F32)
            v1[s, pl.ds(at, 8), :] = cell[8:].astype(BF16).astype(F32)
            return carry

        lax.fori_loop(0, 2 * toks // BLK, pool_chunk, 0, unroll=16)

    def split_chunk(source, s, dst):
        parts = dot_nn(splitter[...], source)
        k_buf[s, pl.ds(dst, MARGIN), :] = parts[:MARGIN].astype(BF16)
        v_buf[s, pl.ds(dst, MARGIN), :HD] = parts[MARGIN:].astype(BF16)

    def loop_split(i, carry):
        for s in range(seqs):
            for j in range(2):
                chunk = i * 2 + j
                start = pl.multiple_of(chunk * BLK, BLK)
                dst = pl.multiple_of(chunk * MARGIN + MARGIN, MARGIN)
                split_chunk(raw[s, pl.ds(start, BLK), :], s, dst)
        return carry

    split_steps = toks // BLK
    split_first = jnp.where(first_half, split_steps, 0)

    pool_row = iota((CELL, 2 * cells), 0)
    pool_col = iota((CELL, 2 * cells), 1)
    pool_two = jnp.where(pool_col // CELL == pool_row, 1.0 / CELL, 0.0).astype(BF16)
    for s in range(seqs):
        ones_kv = jnp.concatenate(
            [k1[s, 32 : 32 + cells, :], v1[s, 32 : 32 + cells, :]], axis=0
        ).astype(BF16)
        pair[core, s] = dot_nn(pool_two, ones_kv).astype(BF16)
    pair_copy = pltpu.make_async_remote_copy(
        src_ref=pair.at[core],
        dst_ref=pair.at[core],
        send_sem=pair_ssem,
        recv_sem=pair_rsem,
        device_id=(me + 1 - 2 * core, head),
        device_id_type=MESH,
    )
    for side in range(2):
        at = 32 if side == 0 else cells
        for s in range(seqs):
            cells_send[side, s, :32, :] = k1[s, at : at + 32, :].astype(BF16)
            cells_send[side, s, 32:, :] = v1[s, at : at + 32, :].astype(BF16)

    def cube_copy(slot):
        target = chip + 2 - core - slot
        return pltpu.make_async_remote_copy(
            src_ref=pair,
            dst_ref=cube_recv.at[slot],
            send_sem=cube_ssem.at[slot],
            recv_sem=cube_rsem.at[slot],
            device_id=(target * 2 + core, head),
            device_id_type=MESH,
        )

    def cube_goes(slot):
        target = chip + 2 - core - slot
        return (target >= 0) & (target < cubes) & (slot != 2 - core)

    def cube_comes(slot):
        source = chip - 2 + core + slot
        return (source >= 0) & (source < cubes) & (slot != 2 - core)

    def third_copy(k):
        return pltpu.make_async_remote_copy(
            src_ref=third_send,
            dst_ref=third.at[pl.ds((cubes - 1 - k) * 8, 8), :],
            send_sem=third_ssem.at[k],
            recv_sem=third_rsem.at[cubes - 1 - k],
            device_id=((chip + k) % cubes * 2 + core, head),
            device_id_type=MESH,
        )

    lane = iota((1, EXTRA), 1)
    ones_tile = jnp.ones((EXTRA, HD), BF16)
    eye = iota((HD, HD), 0) == iota((HD, HD), 1)

    def extra_bias(b):
        start = dev_start + b * BLK
        first_lo = start - 2 * BLK
        first_hi = start + 3 * BLK
        second_lo = (first_lo + CUBE) // CUBE * CUBE - 2 * CUBE
        second_hi = (first_hi + CUBE - 1) // CUBE * CUBE + CUBE
        one_pos = jnp.where(
            lane < LOW, first_lo + lane * CELL, start + 384 + (lane - LOW) * CELL
        )
        two_pos = ((chip - 2 + core) * 16 + lane - 2 * LOW) * BLK
        third_slot = lane - 112
        third_cube = (chip + 1 + third_slot) % cubes
        three_pos = third_cube * CUBE
        one_ok = (one_pos >= 0) & (one_pos < seq_len)
        two_ok = (
            (two_pos >= 0)
            & (two_pos < seq_len)
            & (two_pos >= second_lo)
            & (two_pos < second_hi)
            & ((two_pos < first_lo) | (two_pos >= first_hi))
        )
        three_ok = (third_slot < cubes - 1) & (
            (three_pos < second_lo) | (three_pos >= second_hi)
        )
        return jnp.where(
            lane < 2 * LOW,
            jnp.where(one_ok, LEVEL_STEP, NEG),
            jnp.where(
                lane < 112,
                jnp.where(two_ok, 2 * LEVEL_STEP, NEG),
                jnp.where(three_ok, 3 * LEVEL_STEP, NEG),
            ),
        )

    def near_bias(b):
        pos = dev_start + b * BLK - MARGIN + iota((1, NEAR), 1)
        return jnp.where((pos >= 0) & (pos < seq_len), 0.0, NEG)

    def near_scores(s, b):
        at = pl.multiple_of(b * BLK, BLK)
        return dot_nt(q_buf[s, pl.ds(at, BLK), :], k_buf[s, pl.ds(at, NEAR), :])

    def extra_scores(s, b, bias):
        at = pl.multiple_of(b * BLK, BLK)
        return dot_nt(q_buf[s, pl.ds(at, BLK), :], extras(k1, k23, s, b)) + bias

    def near_values(s, b):
        return v_buf[s, pl.ds(pl.multiple_of(b * BLK, BLK), NEAR), :]

    def extra_values(s, b):
        return jnp.concatenate([extras(v1, v23, s, b), ones_tile], axis=1)

    def weigh(score, top):
        return jnp.exp2((score - top) * EXP_SCALE).astype(BF16)

    def extras(one, rest, s, b):
        cell_at = pl.multiple_of(b * CELL, CELL)
        return jnp.concatenate(
            [
                one[s, pl.ds(cell_at, LOW), :],
                one[s, pl.ds(pl.multiple_of(cell_at + 56, 8), LOW), :],
                rest[s],
            ],
            axis=0,
        ).astype(BF16)

    def near_part(b, place):
        scores = [near_scores(s, b) for s in range(seqs)]
        tops = [jnp.max(score, axis=1, keepdims=True) for score in scores]
        for s in range(seqs):
            near_out[place, s] = dot_nn(weigh(scores[s], tops[s]), near_values(s, b))
            near_top[place, s] = jnp.broadcast_to(tops[s], (BLK, HD))

    def finish(s, b, place, summed, row_total):
        at = pl.multiple_of(b * BLK, BLK)
        result = (summed / row_total).astype(BF16)
        att[s, pl.ds(at, BLK), :] = result
        wide = result.astype(F32)
        square = jnp.sum(wide * wide, axis=1, keepdims=True)
        for half in range(2):
            picked = jnp.where(eye, square[half * HD : half * HD + HD], 0.0)
            row = 2 * s + half
            own_sum[place, row : row + 1, :] = jnp.sum(picked, axis=0, keepdims=True)

    def far_part(b, place):
        bias = extra_bias(b)
        scores = [extra_scores(s, b, bias) for s in range(seqs)]
        for s in range(seqs):
            near = near_top[place, s]
            top = jnp.maximum(near, jnp.max(scores[s], axis=1, keepdims=True))
            shrink = jnp.exp2((near - top) * EXP_SCALE)
            part = dot_nn(weigh(scores[s], top), extra_values(s, b))
            summed = near_out[place, s, :, :HD] * shrink + part[:, :HD]
            row_total = near_out[place, s, :, HD:] * shrink + part[:, HD:]
            finish(s, b, place, summed, row_total)

    def whole_part(b, place, edge):
        bias = extra_bias(b)
        near = [near_scores(s, b) for s in range(seqs)]
        if edge:
            outside = near_bias(b)
            near = [score + outside for score in near]
        far = [extra_scores(s, b, bias) for s in range(seqs)]
        tops = [
            jnp.maximum(
                jnp.max(near[s], axis=1, keepdims=True),
                jnp.max(far[s], axis=1, keepdims=True),
            )
            for s in range(seqs)
        ]
        outs = [
            dot_nn(weigh(near[s], tops[s]), near_values(s, b))
            + dot_nn(weigh(far[s], tops[s]), extra_values(s, b))
            for s in range(seqs)
        ]
        for s in range(seqs):
            finish(s, b, place, outs[s][:, :HD], outs[s][:, HD:])

    def sum_copy(part, k):
        places = pl.ds(*parts[part])
        return pltpu.make_async_remote_copy(
            src_ref=own_sum.at[places],
            dst_ref=sums.at[n_head - 1 - k, places],
            send_sem=sum_ssem.at[part, k],
            recv_sem=sum_rsem.at[part, n_head - 1 - k],
            device_id=(me, (head + k) % n_head),
            device_id_type=MESH,
        )

    def block_at(place):
        inner_end = blocks - 4
        return jnp.where(
            place < inner_end,
            place + 2,
            jnp.where(
                place < inner_end + 2,
                1 + (place - inner_end) * (blocks - 3),
                (place - inner_end - 2) * (blocks - 1),
            ),
        )

    def normalize(place, carry):
        b = block_at(place)
        acc = own_sum[place]
        for k in range(n_head - 1):
            acc = acc + sums[k, place]
        scale = jnp.transpose(1.0 / jnp.sqrt(acc / (HD * n_head) + 1e-06))
        gain = gain_ref[...]
        for s in range(seqs):
            for half in range(2):
                at = pl.multiple_of(b * BLK + half * HD, HD)
                column = scale[:, 2 * s + half : 2 * s + half + 1]
                wide = att[s, pl.ds(at, HD), :].astype(F32)
                att[s, pl.ds(at, HD), :] = (wide * column * gain).astype(BF16)
        return carry

    def loop_near(place, carry):
        near_part(block_at(place), place)
        return carry

    def loop_far(place, carry):
        far_part(block_at(place), place)
        return carry

    def loop_whole(place, carry):
        whole_part(block_at(place), place, False)
        return carry

    def loop_edge(place, carry):
        whole_part(block_at(place), place, True)
        return carry

    def q_wait():
        for s in range(seqs):
            pltpu.make_async_copy(q_hbm.at[s], q_buf.at[s], q_sem.at[s]).wait()

    q_wait()
    lax.fori_loop(0, split_first, loop_split, 0)
    lax.fori_loop(0, early, loop_near, 0)
    pl.semaphore_wait(barrier, cubes + n_head - 1 + outer_there.astype(jnp.int32))
    pair_copy.start()
    lax.fori_loop(split_first, split_steps, loop_split, 0)
    pair_copy.wait()
    for s in range(seqs):
        both = pair[0, s].astype(F32) + pair[1, s].astype(F32)
        for half in range(2):
            mean = jnp.sum(both[8 * half : 8 * half + 8], axis=0, keepdims=True) / CELL
            third_send[2 * s + half : 2 * s + half + 1, :] = mean.astype(BF16).astype(F32)

    for k in range(1, cubes):
        third_copy(k).start()
    for slot in range(4):

        @pl.when(cube_goes(slot))
        def _(slot=slot):
            cube_copy(slot).start()

    for side in range(2):

        @pl.when(there[side])
        def _(side=side):
            cells_copy(side).start()
            token_copy(side).start()

    lax.fori_loop(early, two_pass, loop_near, 0)

    for side in range(2):

        @pl.when(there[side])
        def _(side=side):
            cells_copy(1 - side).wait_recv()
            at = 0 if side == 0 else 32 + cells
            for s in range(seqs):
                k1[s, at : at + 32, :] = cells_recv[side, s, :32, :].astype(F32)
                v1[s, at : at + 32, :] = cells_recv[side, s, 32:, :].astype(F32)

    for k in range(1, cubes):
        third_copy(k).wait_recv()
    for s in range(seqs):
        k23[s, 64:, :] = third[pl.ds(2 * s, 16, stride=8), :]
        v23[s, 64:, :] = third[pl.ds(2 * s + 1, 16, stride=8), :]
    for slot in range(4):
        for half in range(2):
            at = slot * 16 + half * 8

            @pl.when(slot == 2 - core)
            def _(half=half, at=at):
                for s in range(seqs):
                    tile = pair[half, s].astype(F32)
                    k23[s, at : at + 8, :] = tile[:8]
                    v23[s, at : at + 8, :] = tile[8:]

            @pl.when(cube_comes(slot))
            def _(slot=slot, half=half, at=at):
                if half == 0:
                    cube_copy(slot).wait_recv()
                for s in range(seqs):
                    tile = cube_recv[slot, half, s].astype(F32)
                    k23[s, at : at + 8, :] = tile[:8]
                    v23[s, at : at + 8, :] = tile[8:]

    lax.fori_loop(0, two_pass, loop_far, 0)
    lax.fori_loop(two_pass, blocks - 2, loop_whole, 0)
    for k in range(1, n_head):
        sum_copy(0, k).start()

    for side in range(2):

        @pl.when(there[side])
        def _(side=side):
            token_copy(1 - side).wait_recv()
            at = 0 if side == 0 else MARGIN + toks
            for s in range(seqs):
                split_chunk(tok_recv[side, s], s, at)

    lax.fori_loop(blocks - 2, blocks, loop_edge, 0)
    for k in range(1, n_head):
        sum_copy(1, k).start()
    for k in range(1, n_head):
        sum_copy(0, k).wait_recv()
    lax.fori_loop(0, blocks - 2, normalize, 0)
    for k in range(1, n_head):
        sum_copy(1, k).wait_recv()
    lax.fori_loop(blocks - 2, blocks, normalize, 0)

    for part in range(2):
        for k in range(1, n_head):
            sum_copy(part, k).wait_send()
    for side in range(2):

        @pl.when(there[side])
        def _(side=side):
            token_copy(side).wait_send()
            cells_copy(side).wait_send()

    for slot in range(4):

        @pl.when(cube_goes(slot))
        def _(slot=slot):
            cube_copy(slot).wait_send()

    for k in range(1, cubes):
        third_copy(k).wait_send()


def attention(queries, pairs, gain, n_seq, n_head):
    seqs, toks, _ = queries.shape
    blocks = toks // BLK
    cells = toks // CELL
    cubes = n_seq // 2
    assert toks == CUBE // 2 and cubes <= 16 and 2 * seqs <= 8
    vmem = pltpu.VMEM
    dma = pltpu.SemaphoreType.DMA
    hbm = pl.BlockSpec(memory_space=pl.ANY)
    return pl.pallas_call(
        functools.partial(fmm_kernel, n_seq, n_head),
        out_shape=vmem((seqs, toks, HD), BF16),
        in_specs=[hbm, hbm, pl.BlockSpec(memory_space=vmem)],
        out_specs=pl.BlockSpec(memory_space=vmem),
        scratch_shapes=[
            vmem((seqs, 2 * toks, HD), BF16),
            vmem((seqs, toks, HD), BF16),
            vmem((seqs, toks + BLK, HD), BF16),
            vmem((seqs, toks + BLK, 2 * HD), BF16),
            vmem((seqs, cells + 64, HD), F32),
            vmem((seqs, cells + 64, HD), F32),
            vmem((seqs, 80, HD), F32),
            vmem((seqs, 80, HD), F32),
            vmem((2, seqs, BLK, HD), BF16),
            vmem((2, seqs, 64, HD), BF16),
            vmem((2, seqs, 64, HD), BF16),
            vmem((2, seqs, CELL, HD), BF16),
            vmem((4, 2, seqs, CELL, HD), BF16),
            vmem((8, HD), F32),
            vmem((16 * 8, HD), F32),
            vmem((max(TWO_PASS), seqs, BLK, 2 * HD), F32),
            vmem((max(TWO_PASS), seqs, BLK, HD), F32),
            vmem((blocks, 8, HD), F32),
            vmem((n_head - 1, blocks, 8, HD), F32),
            vmem((BLK, BLK), BF16),
            dma((seqs,)),
            dma((seqs,)),
            dma((2,)),
            dma((2,)),
            dma((2,)),
            dma((2,)),
            dma(()),
            dma(()),
            dma((4,)),
            dma((4,)),
            dma((16,)),
            dma((16,)),
            dma((2, n_head)),
            dma((2, n_head)),
        ],
        compiler_params=pltpu.CompilerParams(
            collective_id=0, has_side_effects=True, vmem_limit_bytes=61 * 2**20
        ),
        cost_estimate=pl.CostEstimate(
            flops=4 * seqs * toks * 640 * HD,
            bytes_accessed=8 * seqs * toks * HD,
            transcendentals=seqs * toks * 640,
        ),
    )(queries, pairs, gain)


def on_device(n_seq, n_head, queries, keys_values, norm_gain):
    seqs, toks, width = queries.shape
    pairs = keys_values.reshape(seqs, 2 * toks, width)
    return attention(queries, pairs, norm_gain.reshape(1, HD), n_seq, n_head)


def solution(mesh):
    n_seq, n_head = mesh.shape["seq"], mesh.shape["head"]
    in_specs = (P(None, "seq", "head"), P(None, "seq", None, "head"), P("head"))
    return jax.shard_map(
        functools.partial(on_device, n_seq, n_head),
        mesh=mesh,
        in_specs=in_specs,
        out_specs=P(None, "seq", "head"),
        check_vma=False,
    )
```

```python
import functools
import math

import jax
import jax.numpy as jnp
from jax import lax
from jax.experimental import pallas as pl
from jax.experimental.pallas import tpu as pltpu
from jax.sharding import PartitionSpec as P

HD = 128
CELL = 16
BLK = 256
CUBE = 4096
MARGIN = 128
NEAR = 512
LOW = 24
EXTRA = 128
TWO_PASS = (3, 1)
EARLY = 1
NEG = -1e30
EXP_SCALE = math.log2(math.e) / math.sqrt(HD)
LEVEL_STEP = 2.0 / EXP_SCALE
MESH = pl.DeviceIdType.MESH
F32 = jnp.float32
BF16 = jnp.bfloat16


def dot_nt(a, b):
    return lax.dot_general(a, b, (((1,), (1,)), ((), ())), preferred_element_type=F32)


def dot_nn(a, b):
    return lax.dot_general(a, b, (((1,), (0,)), ((), ())), preferred_element_type=F32)


def iota(shape, dim):
    return lax.broadcasted_iota(jnp.int32, shape, dim)


def split_matrix():
    row = iota((BLK, BLK), 0)
    col = iota((BLK, BLK), 1)
    return (col == 2 * (row % MARGIN) + row // MARGIN).astype(BF16)


def pool_matrix():
    row = iota((CELL, BLK), 0)
    col = iota((CELL, BLK), 1)
    picked = (col // (2 * CELL) == row % 8) & (col % 2 == row // 8)
    return jnp.where(picked, 1.0 / CELL, 0.0).astype(BF16)


def fmm_kernel(
    n_seq,
    n_head,
    q_hbm,
    kv_hbm,
    gain_ref,
    att,
    raw,
    q_buf,
    k_buf,
    v_buf,
    k1,
    v1,
    k23,
    v23,
    tok_recv,
    cells_send,
    cells_recv,
    pair,
    cube_recv,
    third_send,
    third,
    near_out,
    near_top,
    own_sum,
    sums,
    splitter,
    q_sem,
    kv_sem,
    tok_ssem,
    tok_rsem,
    cells_ssem,
    cells_rsem,
    pair_ssem,
    pair_rsem,
    cube_ssem,
    cube_rsem,
    third_ssem,
    third_rsem,
    sum_ssem,
    sum_rsem,
):
    seqs, toks, _ = q_hbm.shape
    blocks = toks // BLK
    cells = toks // CELL
    cubes = n_seq // 2
    seq_len = n_seq * toks
    me = lax.axis_index("seq")
    head = lax.axis_index("head")
    core = me % 2
    chip = me // 2
    dev_start = me * toks
    parts = ((0, blocks - 2), (blocks - 2, 2))
    first_half = me < n_seq // 2
    early = jnp.where(first_half, EARLY, 0)
    two_pass = jnp.where(first_half, *TWO_PASS)
    has_low = me > 0
    has_high = me < n_seq - 1

    for s in range(seqs):
        pltpu.make_async_copy(kv_hbm.at[s], raw.at[s], kv_sem.at[s]).start()
    for s in range(seqs):
        pltpu.make_async_copy(q_hbm.at[s], q_buf.at[s], q_sem.at[s]).start()

    barrier = pltpu.get_barrier_semaphore()

    def greet(seq_id, head_id):
        pl.semaphore_signal(
            barrier, inc=1, device_id=(seq_id, head_id), device_id_type=MESH
        )

    greet(me + 1 - 2 * core, head)
    for k in range(1, cubes):
        greet((chip + k) % cubes * 2 + core, head)
    for k in range(1, n_head):
        greet(me, (head + k) % n_head)
    outer = me - 1 + 2 * core
    outer_there = (outer >= 0) & (outer < n_seq)

    @pl.when(outer_there)
    def _():
        greet(outer, head)

    splitter[...] = split_matrix()
    v_buf[:, :, HD:] = jnp.ones((seqs, toks + BLK, HD), BF16)
    spare = 16 - (cubes - 1)
    third[(cubes - 1) * 8 :, :] = jnp.zeros((spare * 8, HD), F32)
    k23[...] = jnp.zeros_like(k23)
    v23[...] = jnp.zeros_like(v23)

    @pl.when(jnp.logical_not(has_low))
    def _():
        k_buf[:, :MARGIN, :] = jnp.zeros((seqs, MARGIN, HD), BF16)
        v_buf[:, :MARGIN, :HD] = jnp.zeros((seqs, MARGIN, HD), BF16)
        k1[:, :32, :] = jnp.zeros((seqs, 32, HD), F32)
        v1[:, :32, :] = jnp.zeros((seqs, 32, HD), F32)

    @pl.when(jnp.logical_not(has_high))
    def _():
        k_buf[:, MARGIN + toks :, :] = jnp.zeros((seqs, MARGIN, HD), BF16)
        v_buf[:, MARGIN + toks :, :HD] = jnp.zeros((seqs, MARGIN, HD), BF16)
        k1[:, 32 + cells :, :] = jnp.zeros((seqs, 32, HD), F32)
        v1[:, 32 + cells :, :] = jnp.zeros((seqs, 32, HD), F32)


    def token_copy(side):
        rows = pl.ds(0, BLK) if side == 0 else pl.ds(2 * toks - BLK, BLK)
        return pltpu.make_async_remote_copy(
            src_ref=kv_hbm.at[:, rows, :],
            dst_ref=tok_recv.at[1 - side],
            send_sem=tok_ssem.at[side],
            recv_sem=tok_rsem.at[1 - side],
            device_id=(me - 1 if side == 0 else me + 1, head),
            device_id_type=MESH,
        )

    def cells_copy(side):
        return pltpu.make_async_remote_copy(
            src_ref=cells_send.at[side],
            dst_ref=cells_recv.at[1 - side],
            send_sem=cells_ssem.at[side],
            recv_sem=cells_rsem.at[1 - side],
            device_id=(me - 1 if side == 0 else me + 1, head),
            device_id_type=MESH,
        )

    there = (has_low, has_high)
    pooler = pool_matrix()
    for s in range(seqs):
        pltpu.make_async_copy(kv_hbm.at[s], raw.at[s], kv_sem.at[s]).wait()

        def pool_chunk(j, carry, s=s):
            start = pl.multiple_of(j * BLK, BLK)
            cell = dot_nn(pooler, raw[s, pl.ds(start, BLK), :])
            at = pl.multiple_of(j * 8 + 32, 8)
            k1[s, pl.ds(at, 8), :] = cell[:8].astype(BF16).astype(F32)
            v1[s, pl.ds(at, 8), :] = cell[8:].astype(BF16).astype(F32)
            return carry

        lax.fori_loop(0, 2 * toks // BLK, pool_chunk, 0, unroll=16)

    def split_chunks(sources, places):
        parts = dot_nn(splitter[...], jnp.concatenate(sources, axis=1))
        for i, (s, dst) in enumerate(places):
            mine = parts[:, i * HD : i * HD + HD].astype(BF16)
            k_buf[s, pl.ds(dst, MARGIN), :] = mine[:MARGIN]
            v_buf[s, pl.ds(dst, MARGIN), :HD] = mine[MARGIN:]

    def loop_split(i, carry):
        for s in range(seqs):
            start = pl.multiple_of(i * 2 * BLK, 2 * BLK)
            dst = pl.multiple_of(i * BLK + MARGIN, MARGIN)
            split_chunks(
                [raw[s, pl.ds(start, BLK), :], raw[s, pl.ds(start + BLK, BLK), :]],
                [(s, dst), (s, dst + MARGIN)],
            )
        return carry

    split_steps = toks // BLK
    split_first = jnp.where(first_half, split_steps, 0)

    pool_row = iota((CELL, 2 * cells), 0)
    pool_col = iota((CELL, 2 * cells), 1)
    pool_two = jnp.where(pool_col // CELL == pool_row, 1.0 / CELL, 0.0).astype(BF16)
    for s in range(seqs):
        ones_kv = jnp.concatenate(
            [k1[s, 32 : 32 + cells, :], v1[s, 32 : 32 + cells, :]], axis=0
        ).astype(BF16)
        pair[core, s] = dot_nn(pool_two, ones_kv).astype(BF16)
    pair_copy = pltpu.make_async_remote_copy(
        src_ref=pair.at[core],
        dst_ref=pair.at[core],
        send_sem=pair_ssem,
        recv_sem=pair_rsem,
        device_id=(me + 1 - 2 * core, head),
        device_id_type=MESH,
    )
    for side in range(2):
        at = 32 if side == 0 else cells
        for s in range(seqs):
            cells_send[side, s, :32, :] = k1[s, at : at + 32, :].astype(BF16)
            cells_send[side, s, 32:, :] = v1[s, at : at + 32, :].astype(BF16)

    def cube_copy(slot):
        target = chip + 2 - core - slot
        return pltpu.make_async_remote_copy(
            src_ref=pair,
            dst_ref=cube_recv.at[slot],
            send_sem=cube_ssem.at[slot],
            recv_sem=cube_rsem.at[slot],
            device_id=(target * 2 + core, head),
            device_id_type=MESH,
        )

    def cube_goes(slot):
        target = chip + 2 - core - slot
        return (target >= 0) & (target < cubes) & (slot != 2 - core)

    def cube_comes(slot):
        source = chip - 2 + core + slot
        return (source >= 0) & (source < cubes) & (slot != 2 - core)

    def third_copy(k):
        return pltpu.make_async_remote_copy(
            src_ref=third_send,
            dst_ref=third.at[pl.ds((cubes - 1 - k) * 8, 8), :],
            send_sem=third_ssem.at[k],
            recv_sem=third_rsem.at[cubes - 1 - k],
            device_id=((chip + k) % cubes * 2 + core, head),
            device_id_type=MESH,
        )

    lane = iota((1, EXTRA), 1)
    ones_tile = jnp.ones((EXTRA, HD), BF16)
    eye = iota((HD, HD), 0) == iota((HD, HD), 1)

    def extra_bias(b):
        start = dev_start + b * BLK
        first_lo = start - 2 * BLK
        first_hi = start + 3 * BLK
        second_lo = (first_lo + CUBE) // CUBE * CUBE - 2 * CUBE
        second_hi = (first_hi + CUBE - 1) // CUBE * CUBE + CUBE
        one_pos = jnp.where(
            lane < LOW, first_lo + lane * CELL, start + 384 + (lane - LOW) * CELL
        )
        two_pos = ((chip - 2 + core) * 16 + lane - 2 * LOW) * BLK
        third_slot = lane - 112
        third_cube = (chip + 1 + third_slot) % cubes
        three_pos = third_cube * CUBE
        one_ok = (one_pos >= 0) & (one_pos < seq_len)
        two_ok = (
            (two_pos >= 0)
            & (two_pos < seq_len)
            & (two_pos >= second_lo)
            & (two_pos < second_hi)
            & ((two_pos < first_lo) | (two_pos >= first_hi))
        )
        three_ok = (third_slot < cubes - 1) & (
            (three_pos < second_lo) | (three_pos >= second_hi)
        )
        return jnp.where(
            lane < 2 * LOW,
            jnp.where(one_ok, LEVEL_STEP, NEG),
            jnp.where(
                lane < 112,
                jnp.where(two_ok, 2 * LEVEL_STEP, NEG),
                jnp.where(three_ok, 3 * LEVEL_STEP, NEG),
            ),
        )

    def near_bias(b):
        pos = dev_start + b * BLK - MARGIN + iota((1, NEAR), 1)
        return jnp.where((pos >= 0) & (pos < seq_len), 0.0, NEG)

    def near_scores(s, b):
        at = pl.multiple_of(b * BLK, BLK)
        return dot_nt(q_buf[s, pl.ds(at, BLK), :], k_buf[s, pl.ds(at, NEAR), :])

    def extra_scores(s, b, bias):
        at = pl.multiple_of(b * BLK, BLK)
        return dot_nt(q_buf[s, pl.ds(at, BLK), :], extras(k1, k23, s, b)) + bias

    def near_values(s, b):
        return v_buf[s, pl.ds(pl.multiple_of(b * BLK, BLK), NEAR), :]

    def extra_values(s, b):
        return jnp.concatenate([extras(v1, v23, s, b), ones_tile], axis=1)

    def weigh(score, top):
        return jnp.exp2((score - top) * EXP_SCALE).astype(BF16)

    def extras(one, rest, s, b):
        cell_at = pl.multiple_of(b * CELL, CELL)
        return jnp.concatenate(
            [
                one[s, pl.ds(cell_at, LOW), :],
                one[s, pl.ds(pl.multiple_of(cell_at + 56, 8), LOW), :],
                rest[s],
            ],
            axis=0,
        ).astype(BF16)

    def items_of(places):
        return [(s, block_at(place), place) for place in places for s in range(seqs)]

    def near_part(items):
        scores = [near_scores(s, b) for s, b, _ in items]
        tops = [jnp.max(score, axis=1, keepdims=True) for score in scores]
        for (s, b, place), score, top in zip(items, scores, tops):
            near_out[place, s] = dot_nn(weigh(score, top), near_values(s, b))
            near_top[place, s] = jnp.broadcast_to(top, (BLK, HD))

    def finish(s, b, place, summed, row_total):
        at = pl.multiple_of(b * BLK, BLK)
        result = (summed / row_total).astype(BF16)
        att[s, pl.ds(at, BLK), :] = result
        wide = result.astype(F32)
        square = jnp.sum(wide * wide, axis=1, keepdims=True)
        for half in range(2):
            picked = jnp.where(eye, square[half * HD : half * HD + HD], 0.0)
            row = 2 * s + half
            own_sum[place, row : row + 1, :] = jnp.sum(picked, axis=0, keepdims=True)

    def far_part(items):
        scores = [extra_scores(s, b, extra_bias(b)) for s, b, _ in items]
        tops = [
            jnp.maximum(near_top[place, s], jnp.max(score, axis=1, keepdims=True))
            for (s, _, place), score in zip(items, scores)
        ]
        parts = [
            dot_nn(weigh(score, top), extra_values(s, b))
            for (s, b, _), score, top in zip(items, scores, tops)
        ]
        for (s, b, place), part, top in zip(items, parts, tops):
            shrink = jnp.exp2((near_top[place, s] - top) * EXP_SCALE)
            summed = near_out[place, s, :, :HD] * shrink + part[:, :HD]
            row_total = near_out[place, s, :, HD:] * shrink + part[:, HD:]
            finish(s, b, place, summed, row_total)

    def whole_part(items, edge):
        near = [near_scores(s, b) for s, b, _ in items]
        if edge:
            near = [x + near_bias(b) for x, (_, b, _) in zip(near, items)]
        far = [extra_scores(s, b, extra_bias(b)) for s, b, _ in items]
        tops = [
            jnp.maximum(
                jnp.max(x, axis=1, keepdims=True), jnp.max(y, axis=1, keepdims=True)
            )
            for x, y in zip(near, far)
        ]
        outs = [
            dot_nn(weigh(x, top), near_values(s, b))
            + dot_nn(weigh(y, top), extra_values(s, b))
            for (s, b, _), x, y, top in zip(items, near, far, tops)
        ]
        for (s, b, place), out in zip(items, outs):
            finish(s, b, place, out[:, :HD], out[:, HD:])

    def sum_copy(part, k):
        places = pl.ds(*parts[part])
        return pltpu.make_async_remote_copy(
            src_ref=own_sum.at[places],
            dst_ref=sums.at[n_head - 1 - k, places],
            send_sem=sum_ssem.at[part, k],
            recv_sem=sum_rsem.at[part, n_head - 1 - k],
            device_id=(me, (head + k) % n_head),
            device_id_type=MESH,
        )

    def block_at(place):
        inner_end = blocks - 4
        return jnp.where(
            place < inner_end,
            place + 2,
            jnp.where(
                place < inner_end + 2,
                1 + (place - inner_end) * (blocks - 3),
                (place - inner_end - 2) * (blocks - 1),
            ),
        )

    def normalize(place, carry):
        b = block_at(place)
        acc = own_sum[place]
        for k in range(n_head - 1):
            acc = acc + sums[k, place]
        scale = 1.0 / jnp.sqrt(acc / (HD * n_head) + 1e-06)
        gain = gain_ref[...]
        for s in range(seqs):
            for half in range(2):
                at = pl.multiple_of(b * BLK + half * HD, HD)
                row = 2 * s + half
                picked = jnp.where(eye, scale[row : row + 1], 0.0)
                column = jnp.sum(picked, axis=1, keepdims=True)
                wide = att[s, pl.ds(at, HD), :].astype(F32)
                att[s, pl.ds(at, HD), :] = (wide * column * gain).astype(BF16)
        return carry

    def loop_near(i, carry):
        near_part(items_of((2 * i, 2 * i + 1)))
        return carry

    def loop_far(i, carry):
        far_part(items_of((2 * i, 2 * i + 1)))
        return carry

    def loop_whole(i, carry):
        whole_part(items_of((2 * i, 2 * i + 1)), False)
        return carry

    def loop_edge(i, carry):
        whole_part(items_of((2 * i, 2 * i + 1)), True)
        return carry

    def q_wait():
        for s in range(seqs):
            pltpu.make_async_copy(q_hbm.at[s], q_buf.at[s], q_sem.at[s]).wait()

    lax.fori_loop(0, split_first, loop_split, 0)
    q_wait()
    lax.fori_loop(0, early, loop_near, 0)
    pl.semaphore_wait(barrier, cubes + n_head - 1 + outer_there.astype(jnp.int32))
    pair_copy.start()
    lax.fori_loop(split_first, split_steps, loop_split, 0)
    pair_copy.wait()
    for s in range(seqs):
        both = pair[0, s].astype(F32) + pair[1, s].astype(F32)
        for half in range(2):
            mean = jnp.sum(both[8 * half : 8 * half + 8], axis=0, keepdims=True) / CELL
            third_send[2 * s + half : 2 * s + half + 1, :] = mean.astype(BF16).astype(F32)

    for k in range(1, cubes):
        third_copy(k).start()
    for slot in range(4):

        @pl.when(cube_goes(slot))
        def _(slot=slot):
            cube_copy(slot).start()

    for side in range(2):

        @pl.when(there[side])
        def _(side=side):
            cells_copy(side).start()
            token_copy(side).start()

    lax.fori_loop(early, two_pass, loop_near, 0)

    for side in range(2):

        @pl.when(there[side])
        def _(side=side):
            cells_copy(1 - side).wait_recv()
            at = 0 if side == 0 else 32 + cells
            for s in range(seqs):
                k1[s, at : at + 32, :] = cells_recv[side, s, :32, :].astype(F32)
                v1[s, at : at + 32, :] = cells_recv[side, s, 32:, :].astype(F32)

    for k in range(1, cubes):
        third_copy(k).wait_recv()
    for s in range(seqs):
        k23[s, 64:, :] = third[pl.ds(2 * s, 16, stride=8), :]
        v23[s, 64:, :] = third[pl.ds(2 * s + 1, 16, stride=8), :]
    for slot in range(4):
        for half in range(2):
            at = slot * 16 + half * 8

            @pl.when(slot == 2 - core)
            def _(half=half, at=at):
                for s in range(seqs):
                    tile = pair[half, s].astype(F32)
                    k23[s, at : at + 8, :] = tile[:8]
                    v23[s, at : at + 8, :] = tile[8:]

            @pl.when(cube_comes(slot))
            def _(slot=slot, half=half, at=at):
                if half == 0:
                    cube_copy(slot).wait_recv()
                for s in range(seqs):
                    tile = cube_recv[slot, half, s].astype(F32)
                    k23[s, at : at + 8, :] = tile[:8]
                    v23[s, at : at + 8, :] = tile[8:]

    lax.fori_loop(0, two_pass, loop_far, 0)
    lax.fori_loop(two_pass, blocks // 2 - 1, loop_whole, 0)
    for k in range(1, n_head):
        sum_copy(0, k).start()

    for side in range(2):

        @pl.when(there[side])
        def _(side=side):
            token_copy(1 - side).wait_recv()
            at = 0 if side == 0 else MARGIN + toks
            for s in range(0, seqs, 2):
                pair_of = range(s, min(s + 2, seqs))
                split_chunks(
                    [tok_recv[side, i] for i in pair_of], [(i, at) for i in pair_of]
                )

    lax.fori_loop(blocks // 2 - 1, blocks // 2, loop_edge, 0)
    for k in range(1, n_head):
        sum_copy(1, k).start()
    for k in range(1, n_head):
        sum_copy(0, k).wait_recv()
    lax.fori_loop(0, blocks - 2, normalize, 0)
    for k in range(1, n_head):
        sum_copy(1, k).wait_recv()
    lax.fori_loop(blocks - 2, blocks, normalize, 0)

    for part in range(2):
        for k in range(1, n_head):
            sum_copy(part, k).wait_send()
    for side in range(2):

        @pl.when(there[side])
        def _(side=side):
            token_copy(side).wait_send()
            cells_copy(side).wait_send()

    for slot in range(4):

        @pl.when(cube_goes(slot))
        def _(slot=slot):
            cube_copy(slot).wait_send()

    for k in range(1, cubes):
        third_copy(k).wait_send()


def attention(queries, pairs, gain, n_seq, n_head):
    seqs, toks, _ = queries.shape
    blocks = toks // BLK
    cells = toks // CELL
    cubes = n_seq // 2
    assert toks == CUBE // 2 and cubes <= 16 and 2 * seqs <= 8
    vmem = pltpu.VMEM
    dma = pltpu.SemaphoreType.DMA
    hbm = pl.BlockSpec(memory_space=pl.ANY)
    return pl.pallas_call(
        functools.partial(fmm_kernel, n_seq, n_head),
        out_shape=vmem((seqs, toks, HD), BF16),
        in_specs=[hbm, hbm, pl.BlockSpec(memory_space=vmem)],
        out_specs=pl.BlockSpec(memory_space=vmem),
        scratch_shapes=[
            vmem((seqs, 2 * toks, HD), BF16),
            vmem((seqs, toks, HD), BF16),
            vmem((seqs, toks + BLK, HD), BF16),
            vmem((seqs, toks + BLK, 2 * HD), BF16),
            vmem((seqs, cells + 64, HD), F32),
            vmem((seqs, cells + 64, HD), F32),
            vmem((seqs, 80, HD), F32),
            vmem((seqs, 80, HD), F32),
            vmem((2, seqs, BLK, HD), BF16),
            vmem((2, seqs, 64, HD), BF16),
            vmem((2, seqs, 64, HD), BF16),
            vmem((2, seqs, CELL, HD), BF16),
            vmem((4, 2, seqs, CELL, HD), BF16),
            vmem((8, HD), F32),
            vmem((16 * 8, HD), F32),
            vmem((2 * max(TWO_PASS), seqs, BLK, 2 * HD), F32),
            vmem((2 * max(TWO_PASS), seqs, BLK, HD), F32),
            vmem((blocks, 8, HD), F32),
            vmem((n_head - 1, blocks, 8, HD), F32),
            vmem((BLK, BLK), BF16),
            dma((seqs,)),
            dma((seqs,)),
            dma((2,)),
            dma((2,)),
            dma((2,)),
            dma((2,)),
            dma(()),
            dma(()),
            dma((4,)),
            dma((4,)),
            dma((16,)),
            dma((16,)),
            dma((2, n_head)),
            dma((2, n_head)),
        ],
        compiler_params=pltpu.CompilerParams(
            collective_id=0, has_side_effects=True, vmem_limit_bytes=61 * 2**20
        ),
        cost_estimate=pl.CostEstimate(
            flops=4 * seqs * toks * 640 * HD,
            bytes_accessed=8 * seqs * toks * HD,
            transcendentals=seqs * toks * 640,
        ),
    )(queries, pairs, gain)


def on_device(n_seq, n_head, queries, keys_values, norm_gain):
    seqs, toks, width = queries.shape
    pairs = keys_values.reshape(seqs, 2 * toks, width)
    return attention(queries, pairs, norm_gain.reshape(1, HD), n_seq, n_head)


def solution(mesh):
    n_seq, n_head = mesh.shape["seq"], mesh.shape["head"]
    in_specs = (P(None, "seq", "head"), P(None, "seq", None, "head"), P("head"))
    return jax.shard_map(
        functools.partial(on_device, n_seq, n_head),
        mesh=mesh,
        in_specs=in_specs,
        out_specs=P(None, "seq", "head"),
        check_vma=False,
    )
```

```python
import functools
import math

import jax
import jax.numpy as jnp
from jax import lax
from jax.experimental import pallas as pl
from jax.experimental.pallas import tpu as pltpu
from jax.sharding import PartitionSpec as P

HD = 128
CELL = 16
BLK = 256
CUBE = 4096
MARGIN = 128
NEAR = 512
LOW = 24
EXTRA = 128
TWO_PASS = (3, 2)
EARLY = 1
SPLIT_THEN = 3
NEG = -1e30
EXP_SCALE = math.log2(math.e) / math.sqrt(HD)
LEVEL_STEP = 2.0 / EXP_SCALE
MESH = pl.DeviceIdType.MESH
F32 = jnp.float32
BF16 = jnp.bfloat16


def dot_nt(a, b):
    return lax.dot_general(a, b, (((1,), (1,)), ((), ())), preferred_element_type=F32)


def dot_nn(a, b):
    return lax.dot_general(a, b, (((1,), (0,)), ((), ())), preferred_element_type=F32)


def iota(shape, dim):
    return lax.broadcasted_iota(jnp.int32, shape, dim)


def split_matrix():
    row = iota((BLK, BLK), 0)
    col = iota((BLK, BLK), 1)
    return (col == 2 * (row % MARGIN) + row // MARGIN).astype(BF16)


def pool_matrix():
    row = iota((CELL, BLK), 0)
    col = iota((CELL, BLK), 1)
    picked = (col // (2 * CELL) == row % 8) & (col % 2 == row // 8)
    return jnp.where(picked, 1.0 / CELL, 0.0).astype(BF16)


def fmm_kernel(
    n_seq,
    n_head,
    q_hbm,
    kv_hbm,
    gain_ref,
    att,
    raw,
    q_buf,
    k_buf,
    v_buf,
    k1,
    v1,
    k23,
    v23,
    tok_recv,
    cells_send,
    cells_recv,
    pair,
    cube_recv,
    third_send,
    third,
    near_out,
    near_top,
    own_sum,
    sums,
    splitter,
    q_sem,
    kv_sem,
    tok_ssem,
    tok_rsem,
    cells_ssem,
    cells_rsem,
    pair_ssem,
    pair_rsem,
    cube_ssem,
    cube_rsem,
    third_ssem,
    third_rsem,
    sum_ssem,
    sum_rsem,
):
    seqs, toks, _ = q_hbm.shape
    blocks = toks // BLK
    cells = toks // CELL
    cubes = n_seq // 2
    seq_len = n_seq * toks
    me = lax.axis_index("seq")
    head = lax.axis_index("head")
    core = me % 2
    chip = me // 2
    dev_start = me * toks
    parts = ((0, blocks - 2), (blocks - 2, 2))
    first_half = me < n_seq // 2
    early = jnp.where(first_half & (chip % 2 == 0), EARLY, 0)
    two_pass = jnp.where(first_half, *TWO_PASS)
    has_low = me > 0
    has_high = me < n_seq - 1

    for s in range(seqs):
        pltpu.make_async_copy(kv_hbm.at[s], raw.at[s], kv_sem.at[s]).start()
    for s in range(seqs):
        pltpu.make_async_copy(q_hbm.at[s], q_buf.at[s], q_sem.at[s]).start()

    barrier = pltpu.get_barrier_semaphore()

    def greet(seq_id, head_id):
        pl.semaphore_signal(
            barrier, inc=1, device_id=(seq_id, head_id), device_id_type=MESH
        )

    greet(me + 1 - 2 * core, head)
    for k in range(1, cubes):
        greet((chip + k) % cubes * 2 + core, head)
    for k in range(1, n_head):
        greet(me, (head + k) % n_head)
    outer = me - 1 + 2 * core
    outer_there = (outer >= 0) & (outer < n_seq)

    @pl.when(outer_there)
    def _():
        greet(outer, head)

    splitter[...] = split_matrix()
    v_buf[:, :, HD:] = jnp.ones((seqs, toks + BLK, HD), BF16)
    spare = 16 - (cubes - 1)
    third[(cubes - 1) * 8 :, :] = jnp.zeros((spare * 8, HD), F32)
    k23[...] = jnp.zeros_like(k23)
    v23[...] = jnp.zeros_like(v23)

    @pl.when(jnp.logical_not(has_low))
    def _():
        k_buf[:, :MARGIN, :] = jnp.zeros((seqs, MARGIN, HD), BF16)
        v_buf[:, :MARGIN, :HD] = jnp.zeros((seqs, MARGIN, HD), BF16)
        k1[:, :32, :] = jnp.zeros((seqs, 32, HD), F32)
        v1[:, :32, :] = jnp.zeros((seqs, 32, HD), F32)

    @pl.when(jnp.logical_not(has_high))
    def _():
        k_buf[:, MARGIN + toks :, :] = jnp.zeros((seqs, MARGIN, HD), BF16)
        v_buf[:, MARGIN + toks :, :HD] = jnp.zeros((seqs, MARGIN, HD), BF16)
        k1[:, 32 + cells :, :] = jnp.zeros((seqs, 32, HD), F32)
        v1[:, 32 + cells :, :] = jnp.zeros((seqs, 32, HD), F32)


    def token_copy(side):
        rows = pl.ds(0, BLK) if side == 0 else pl.ds(2 * toks - BLK, BLK)
        return pltpu.make_async_remote_copy(
            src_ref=kv_hbm.at[:, rows, :],
            dst_ref=tok_recv.at[1 - side],
            send_sem=tok_ssem.at[side],
            recv_sem=tok_rsem.at[1 - side],
            device_id=(me - 1 if side == 0 else me + 1, head),
            device_id_type=MESH,
        )

    def cells_copy(side):
        return pltpu.make_async_remote_copy(
            src_ref=cells_send.at[side],
            dst_ref=cells_recv.at[1 - side],
            send_sem=cells_ssem.at[side],
            recv_sem=cells_rsem.at[1 - side],
            device_id=(me - 1 if side == 0 else me + 1, head),
            device_id_type=MESH,
        )

    there = (has_low, has_high)
    pooler = pool_matrix()
    for s in range(seqs):
        pltpu.make_async_copy(kv_hbm.at[s], raw.at[s], kv_sem.at[s]).wait()

        def pool_chunk(j, carry, s=s):
            start = pl.multiple_of(j * BLK, BLK)
            cell = dot_nn(pooler, raw[s, pl.ds(start, BLK), :])
            at = pl.multiple_of(j * 8 + 32, 8)
            k1[s, pl.ds(at, 8), :] = cell[:8].astype(BF16).astype(F32)
            v1[s, pl.ds(at, 8), :] = cell[8:].astype(BF16).astype(F32)
            return carry

        lax.fori_loop(0, 2 * toks // BLK, pool_chunk, 0, unroll=16)

    def split_chunks(sources, places):
        parts = dot_nn(splitter[...], jnp.concatenate(sources, axis=1))
        for i, (s, dst) in enumerate(places):
            mine = parts[:, i * HD : i * HD + HD].astype(BF16)
            k_buf[s, pl.ds(dst, MARGIN), :] = mine[:MARGIN]
            v_buf[s, pl.ds(dst, MARGIN), :HD] = mine[MARGIN:]

    def loop_split(i, carry):
        for s in range(seqs):
            start = pl.multiple_of(i * 2 * BLK, 2 * BLK)
            dst = pl.multiple_of(i * BLK + MARGIN, MARGIN)
            split_chunks(
                [raw[s, pl.ds(start, BLK), :], raw[s, pl.ds(start + BLK, BLK), :]],
                [(s, dst), (s, dst + MARGIN)],
            )
        return carry

    split_steps = toks // BLK
    split_first = jnp.where(first_half, split_steps, 0)

    pool_row = iota((CELL, 2 * cells), 0)
    pool_col = iota((CELL, 2 * cells), 1)
    pool_two = jnp.where(pool_col // CELL == pool_row, 1.0 / CELL, 0.0).astype(BF16)
    for s in range(seqs):
        ones_kv = jnp.concatenate(
            [k1[s, 32 : 32 + cells, :], v1[s, 32 : 32 + cells, :]], axis=0
        ).astype(BF16)
        pair[core, s] = dot_nn(pool_two, ones_kv).astype(BF16)
    pair_copy = pltpu.make_async_remote_copy(
        src_ref=pair.at[core],
        dst_ref=pair.at[core],
        send_sem=pair_ssem,
        recv_sem=pair_rsem,
        device_id=(me + 1 - 2 * core, head),
        device_id_type=MESH,
    )
    for side in range(2):
        at = 32 if side == 0 else cells
        for s in range(seqs):
            cells_send[side, s, :32, :] = k1[s, at : at + 32, :].astype(BF16)
            cells_send[side, s, 32:, :] = v1[s, at : at + 32, :].astype(BF16)

    def cube_copy(slot):
        target = chip + 2 - core - slot
        return pltpu.make_async_remote_copy(
            src_ref=pair,
            dst_ref=cube_recv.at[slot],
            send_sem=cube_ssem.at[slot],
            recv_sem=cube_rsem.at[slot],
            device_id=(target * 2 + core, head),
            device_id_type=MESH,
        )

    def cube_goes(slot):
        target = chip + 2 - core - slot
        return (target >= 0) & (target < cubes) & (slot != 2 - core)

    def cube_comes(slot):
        source = chip - 2 + core + slot
        return (source >= 0) & (source < cubes) & (slot != 2 - core)

    def third_copy(k):
        return pltpu.make_async_remote_copy(
            src_ref=third_send,
            dst_ref=third.at[pl.ds((cubes - 1 - k) * 8, 8), :],
            send_sem=third_ssem.at[k],
            recv_sem=third_rsem.at[cubes - 1 - k],
            device_id=((chip + k) % cubes * 2 + core, head),
            device_id_type=MESH,
        )

    lane = iota((1, EXTRA), 1)
    ones_tile = jnp.ones((EXTRA, HD), BF16)
    eye = iota((HD, HD), 0) == iota((HD, HD), 1)

    def extra_bias(b):
        start = dev_start + b * BLK
        first_lo = start - 2 * BLK
        first_hi = start + 3 * BLK
        second_lo = (first_lo + CUBE) // CUBE * CUBE - 2 * CUBE
        second_hi = (first_hi + CUBE - 1) // CUBE * CUBE + CUBE
        one_pos = jnp.where(
            lane < LOW, first_lo + lane * CELL, start + 384 + (lane - LOW) * CELL
        )
        two_pos = ((chip - 2 + core) * 16 + lane - 2 * LOW) * BLK
        third_slot = lane - 112
        third_cube = (chip + 1 + third_slot) % cubes
        three_pos = third_cube * CUBE
        one_ok = (one_pos >= 0) & (one_pos < seq_len)
        two_ok = (
            (two_pos >= 0)
            & (two_pos < seq_len)
            & (two_pos >= second_lo)
            & (two_pos < second_hi)
            & ((two_pos < first_lo) | (two_pos >= first_hi))
        )
        three_ok = (third_slot < cubes - 1) & (
            (three_pos < second_lo) | (three_pos >= second_hi)
        )
        return jnp.where(
            lane < 2 * LOW,
            jnp.where(one_ok, LEVEL_STEP, NEG),
            jnp.where(
                lane < 112,
                jnp.where(two_ok, 2 * LEVEL_STEP, NEG),
                jnp.where(three_ok, 3 * LEVEL_STEP, NEG),
            ),
        )

    def near_scores(s, b):
        at = pl.multiple_of(b * BLK, BLK)
        return dot_nt(q_buf[s, pl.ds(at, BLK), :], k_buf[s, pl.ds(at, NEAR), :])

    def extra_scores(s, b, bias):
        at = pl.multiple_of(b * BLK, BLK)
        return dot_nt(q_buf[s, pl.ds(at, BLK), :], extras(k1, k23, s, b)) + bias

    def near_values(s, b):
        return v_buf[s, pl.ds(pl.multiple_of(b * BLK, BLK), NEAR), :]

    def extra_values(s, b):
        return jnp.concatenate([extras(v1, v23, s, b), ones_tile], axis=1)

    def weigh(score, top):
        return jnp.exp2((score - top) * EXP_SCALE).astype(BF16)

    def extras(one, rest, s, b):
        cell_at = pl.multiple_of(b * CELL, CELL)
        return jnp.concatenate(
            [
                one[s, pl.ds(cell_at, LOW), :],
                one[s, pl.ds(pl.multiple_of(cell_at + 56, 8), LOW), :],
                rest[s],
            ],
            axis=0,
        ).astype(BF16)

    def items_of(places):
        return [(s, block_at(place), place) for place in places for s in range(seqs)]

    def near_part(items):
        scores = [near_scores(s, b) for s, b, _ in items]
        tops = [jnp.max(score, axis=1, keepdims=True) for score in scores]
        for (s, b, place), score, top in zip(items, scores, tops):
            near_out[place, s] = dot_nn(weigh(score, top), near_values(s, b))
            near_top[place, s] = jnp.broadcast_to(top, (BLK, HD))

    def finish(s, b, place, summed, row_total):
        at = pl.multiple_of(b * BLK, BLK)
        result = (summed / row_total).astype(BF16)
        att[s, pl.ds(at, BLK), :] = result
        wide = result.astype(F32)
        square = jnp.sum(wide * wide, axis=1, keepdims=True)
        for half in range(2):
            picked = jnp.where(eye, square[half * HD : half * HD + HD], 0.0)
            row = 2 * s + half
            own_sum[place, row : row + 1, :] = jnp.sum(picked, axis=0, keepdims=True)

    def merge(items, scores, values):
        tops = [
            jnp.maximum(near_top[slot, s], jnp.max(score, axis=1, keepdims=True))
            for (s, _, _, slot), score in zip(items, scores)
        ]
        parts = [
            dot_nn(weigh(score, top), values(s, b))
            for (s, b, _, _), score, top in zip(items, scores, tops)
        ]
        for (s, b, place, slot), part, top in zip(items, parts, tops):
            shrink = jnp.exp2((near_top[slot, s] - top) * EXP_SCALE)
            summed = near_out[slot, s, :, :HD] * shrink + part[:, :HD]
            row_total = near_out[slot, s, :, HD:] * shrink + part[:, HD:]
            finish(s, b, place, summed, row_total)

    def far_part(items):
        scores = [extra_scores(s, b, extra_bias(b)) for s, b, _ in items]
        merge([(s, b, place, place) for s, b, place in items], scores, extra_values)

    def halo_at(b):
        return pl.multiple_of(jnp.where(b == 0, 0, MARGIN + toks), MARGIN)

    def edge_local(items):
        span = NEAR - MARGIN
        near = []
        for s, b, _ in items:
            at = pl.multiple_of(b * BLK, BLK)
            local = pl.multiple_of(at + jnp.where(b == 0, MARGIN, 0), MARGIN)
            keys = k_buf[s, pl.ds(local, span), :]
            near.append(dot_nt(q_buf[s, pl.ds(at, BLK), :], keys))
        far = [extra_scores(s, b, extra_bias(b)) for s, b, _ in items]
        tops = [
            jnp.maximum(
                jnp.max(x, axis=1, keepdims=True), jnp.max(y, axis=1, keepdims=True)
            )
            for x, y in zip(near, far)
        ]
        for (s, b, place), x, y, top in zip(items, near, far, tops):
            at = b * BLK + jnp.where(b == 0, MARGIN, 0)
            values = v_buf[s, pl.ds(pl.multiple_of(at, MARGIN), span), :]
            slot = place - (blocks - 2)
            near_out[slot, s] = dot_nn(weigh(x, top), values) + dot_nn(
                weigh(y, top), extra_values(s, b)
            )
            near_top[slot, s] = jnp.broadcast_to(top, (BLK, HD))

    def halo_scores(s, b):
        at = pl.multiple_of(b * BLK, BLK)
        pos = dev_start + halo_at(b) - MARGIN + iota((1, MARGIN), 1)
        bias = jnp.where((pos >= 0) & (pos < seq_len), 0.0, NEG)
        keys = k_buf[s, pl.ds(halo_at(b), MARGIN), :]
        return dot_nt(q_buf[s, pl.ds(at, BLK), :], keys) + bias

    def halo_values(s, b):
        return v_buf[s, pl.ds(halo_at(b), MARGIN), :]

    def edge_halo(items):
        scores = [halo_scores(s, b) for s, b, _ in items]
        with_slots = [(s, b, place, place - (blocks - 2)) for s, b, place in items]
        merge(with_slots, scores, halo_values)

    def whole_part(items):
        near = [near_scores(s, b) for s, b, _ in items]
        far = [extra_scores(s, b, extra_bias(b)) for s, b, _ in items]
        tops = [
            jnp.maximum(
                jnp.max(x, axis=1, keepdims=True), jnp.max(y, axis=1, keepdims=True)
            )
            for x, y in zip(near, far)
        ]
        outs = [
            dot_nn(weigh(x, top), near_values(s, b))
            + dot_nn(weigh(y, top), extra_values(s, b))
            for (s, b, _), x, y, top in zip(items, near, far, tops)
        ]
        for (s, b, place), out in zip(items, outs):
            finish(s, b, place, out[:, :HD], out[:, HD:])

    def sum_copy(part, k):
        places = pl.ds(*parts[part])
        return pltpu.make_async_remote_copy(
            src_ref=own_sum.at[places],
            dst_ref=sums.at[n_head - 1 - k, places],
            send_sem=sum_ssem.at[part, k],
            recv_sem=sum_rsem.at[part, n_head - 1 - k],
            device_id=(me, (head + k) % n_head),
            device_id_type=MESH,
        )

    def block_at(place):
        inner_end = blocks - 4
        return jnp.where(
            place < inner_end,
            place + 2,
            jnp.where(
                place < inner_end + 2,
                1 + (place - inner_end) * (blocks - 3),
                (place - inner_end - 2) * (blocks - 1),
            ),
        )

    def normalize(place, carry):
        b = block_at(place)
        acc = own_sum[place]
        for k in range(n_head - 1):
            acc = acc + sums[k, place]
        scale = 1.0 / jnp.sqrt(acc / (HD * n_head) + 1e-06)
        gain = gain_ref[...]
        for s in range(seqs):
            for half in range(2):
                at = pl.multiple_of(b * BLK + half * HD, HD)
                row = 2 * s + half
                picked = jnp.where(eye, scale[row : row + 1], 0.0)
                column = jnp.sum(picked, axis=1, keepdims=True)
                wide = att[s, pl.ds(at, HD), :].astype(F32)
                att[s, pl.ds(at, HD), :] = (wide * column * gain).astype(BF16)
        return carry

    def loop_near(i, carry):
        near_part(items_of((2 * i, 2 * i + 1)))
        return carry

    def loop_far(i, carry):
        far_part(items_of((2 * i, 2 * i + 1)))
        return carry

    def loop_whole(i, carry):
        whole_part(items_of((2 * i, 2 * i + 1)))
        return carry

    def loop_local(i, carry):
        edge_local(items_of((2 * i, 2 * i + 1)))
        return carry

    def loop_edge(i, carry):
        edge_halo(items_of((2 * i, 2 * i + 1)))
        return carry

    def q_wait():
        for s in range(seqs):
            pltpu.make_async_copy(q_hbm.at[s], q_buf.at[s], q_sem.at[s]).wait()

    lax.fori_loop(0, split_first, loop_split, 0)

    @pl.when(first_half)
    def _():
        q_wait()

    lax.fori_loop(0, early, loop_near, 0)
    pl.semaphore_wait(barrier, cubes + n_head - 1 + outer_there.astype(jnp.int32))
    pair_copy.start()
    split_then = jnp.where(first_half, split_steps, SPLIT_THEN)
    lax.fori_loop(split_first, split_then, loop_split, 0)
    pair_copy.wait()
    for s in range(seqs):
        both = pair[0, s].astype(F32) + pair[1, s].astype(F32)
        for half in range(2):
            mean = jnp.sum(both[8 * half : 8 * half + 8], axis=0, keepdims=True) / CELL
            third_send[2 * s + half : 2 * s + half + 1, :] = mean.astype(BF16).astype(F32)

    for k in range(1, cubes):
        third_copy(k).start()
    for slot in range(4):

        @pl.when(cube_goes(slot))
        def _(slot=slot):
            cube_copy(slot).start()

    for side in range(2):

        @pl.when(there[side])
        def _(side=side):
            cells_copy(side).start()
            token_copy(side).start()

    lax.fori_loop(split_then, split_steps, loop_split, 0)

    @pl.when(jnp.logical_not(first_half))
    def _():
        q_wait()

    lax.fori_loop(early, two_pass, loop_near, 0)

    for side in range(2):

        @pl.when(there[side])
        def _(side=side):
            cells_copy(1 - side).wait_recv()
            at = 0 if side == 0 else 32 + cells
            for s in range(seqs):
                k1[s, at : at + 32, :] = cells_recv[side, s, :32, :].astype(F32)
                v1[s, at : at + 32, :] = cells_recv[side, s, 32:, :].astype(F32)

    for k in range(1, cubes):
        third_copy(k).wait_recv()
    for s in range(seqs):
        k23[s, 64:, :] = third[pl.ds(2 * s, 16, stride=8), :]
        v23[s, 64:, :] = third[pl.ds(2 * s + 1, 16, stride=8), :]
    for slot in range(4):
        for half in range(2):
            at = slot * 16 + half * 8

            @pl.when(slot == 2 - core)
            def _(half=half, at=at):
                for s in range(seqs):
                    tile = pair[half, s].astype(F32)
                    k23[s, at : at + 8, :] = tile[:8]
                    v23[s, at : at + 8, :] = tile[8:]

            @pl.when(cube_comes(slot))
            def _(slot=slot, half=half, at=at):
                if half == 0:
                    cube_copy(slot).wait_recv()
                for s in range(seqs):
                    tile = cube_recv[slot, half, s].astype(F32)
                    k23[s, at : at + 8, :] = tile[:8]
                    v23[s, at : at + 8, :] = tile[8:]

    lax.fori_loop(0, two_pass, loop_far, 0)
    lax.fori_loop(two_pass, blocks // 2 - 1, loop_whole, 0)
    for k in range(1, n_head):
        sum_copy(0, k).start()

    lax.fori_loop(blocks // 2 - 1, blocks // 2, loop_local, 0)
    for side in range(2):

        @pl.when(there[side])
        def _(side=side):
            token_copy(1 - side).wait_recv()
            at = 0 if side == 0 else MARGIN + toks
            for s in range(0, seqs, 2):
                pair_of = range(s, min(s + 2, seqs))
                split_chunks(
                    [tok_recv[side, i] for i in pair_of], [(i, at) for i in pair_of]
                )

    lax.fori_loop(blocks // 2 - 1, blocks // 2, loop_edge, 0)
    for k in range(1, n_head):
        sum_copy(1, k).start()
    for k in range(1, n_head):
        sum_copy(0, k).wait_recv()
    lax.fori_loop(0, blocks - 2, normalize, 0)
    for k in range(1, n_head):
        sum_copy(1, k).wait_recv()
    lax.fori_loop(blocks - 2, blocks, normalize, 0)

    for part in range(2):
        for k in range(1, n_head):
            sum_copy(part, k).wait_send()
    for side in range(2):

        @pl.when(there[side])
        def _(side=side):
            token_copy(side).wait_send()
            cells_copy(side).wait_send()

    for slot in range(4):

        @pl.when(cube_goes(slot))
        def _(slot=slot):
            cube_copy(slot).wait_send()

    for k in range(1, cubes):
        third_copy(k).wait_send()


def attention(queries, pairs, gain, n_seq, n_head):
    seqs, toks, _ = queries.shape
    blocks = toks // BLK
    cells = toks // CELL
    cubes = n_seq // 2
    assert toks == CUBE // 2 and cubes <= 16 and 2 * seqs <= 8
    vmem = pltpu.VMEM
    dma = pltpu.SemaphoreType.DMA
    hbm = pl.BlockSpec(memory_space=pl.ANY)
    return pl.pallas_call(
        functools.partial(fmm_kernel, n_seq, n_head),
        out_shape=vmem((seqs, toks, HD), BF16),
        in_specs=[hbm, hbm, pl.BlockSpec(memory_space=vmem)],
        out_specs=pl.BlockSpec(memory_space=vmem),
        scratch_shapes=[
            vmem((seqs, 2 * toks, HD), BF16),
            vmem((seqs, toks, HD), BF16),
            vmem((seqs, toks + BLK, HD), BF16),
            vmem((seqs, toks + BLK, 2 * HD), BF16),
            vmem((seqs, cells + 64, HD), F32),
            vmem((seqs, cells + 64, HD), F32),
            vmem((seqs, 80, HD), F32),
            vmem((seqs, 80, HD), F32),
            vmem((2, seqs, BLK, HD), BF16),
            vmem((2, seqs, 64, HD), BF16),
            vmem((2, seqs, 64, HD), BF16),
            vmem((2, seqs, CELL, HD), BF16),
            vmem((4, 2, seqs, CELL, HD), BF16),
            vmem((8, HD), F32),
            vmem((16 * 8, HD), F32),
            vmem((2 * max(TWO_PASS), seqs, BLK, 2 * HD), F32),
            vmem((2 * max(TWO_PASS), seqs, BLK, HD), F32),
            vmem((blocks, 8, HD), F32),
            vmem((n_head - 1, blocks, 8, HD), F32),
            vmem((BLK, BLK), BF16),
            dma((seqs,)),
            dma((seqs,)),
            dma((2,)),
            dma((2,)),
            dma((2,)),
            dma((2,)),
            dma(()),
            dma(()),
            dma((4,)),
            dma((4,)),
            dma((16,)),
            dma((16,)),
            dma((2, n_head)),
            dma((2, n_head)),
        ],
        compiler_params=pltpu.CompilerParams(
            collective_id=0, has_side_effects=True, vmem_limit_bytes=61 * 2**20
        ),
        cost_estimate=pl.CostEstimate(
            flops=4 * seqs * toks * 640 * HD,
            bytes_accessed=8 * seqs * toks * HD,
            transcendentals=seqs * toks * 640,
        ),
    )(queries, pairs, gain)


def on_device(n_seq, n_head, queries, keys_values, norm_gain):
    seqs, toks, width = queries.shape
    pairs = keys_values.reshape(seqs, 2 * toks, width)
    return attention(queries, pairs, norm_gain.reshape(1, HD), n_seq, n_head)


def solution(mesh):
    n_seq, n_head = mesh.shape["seq"], mesh.shape["head"]
    in_specs = (P(None, "seq", "head"), P(None, "seq", None, "head"), P("head"))
    return jax.shard_map(
        functools.partial(on_device, n_seq, n_head),
        mesh=mesh,
        in_specs=in_specs,
        out_specs=P(None, "seq", "head"),
        check_vma=False,
    )
```

```python
import functools
import math

import jax
import jax.numpy as jnp
from jax import lax
from jax.experimental import pallas as pl
from jax.experimental.pallas import tpu as pltpu
from jax.sharding import PartitionSpec as P

HD = 128
CELL = 16
BLK = 256
CUBE = 4096
MARGIN = 128
NEAR = 512
LOW = 24
EXTRA = 128
TWO_PASS = (3, 2)
EARLY = 1
SPLIT_THEN = 3
NEG = -1e30
EXP_SCALE = math.log2(math.e) / math.sqrt(HD)
LEVEL_STEP = 2.0 / EXP_SCALE
MESH = pl.DeviceIdType.MESH
F32 = jnp.float32
BF16 = jnp.bfloat16


def dot_nt(a, b):
    return lax.dot_general(a, b, (((1,), (1,)), ((), ())), preferred_element_type=F32)


def dot_nn(a, b):
    return lax.dot_general(a, b, (((1,), (0,)), ((), ())), preferred_element_type=F32)


def iota(shape, dim):
    return lax.broadcasted_iota(jnp.int32, shape, dim)


def split_matrix():
    row = iota((BLK, BLK), 0)
    col = iota((BLK, BLK), 1)
    return (col == 2 * (row % MARGIN) + row // MARGIN).astype(BF16)


def pool_matrix():
    row = iota((CELL, BLK), 0)
    col = iota((CELL, BLK), 1)
    picked = (col // (2 * CELL) == row % 8) & (col % 2 == row // 8)
    return jnp.where(picked, 1.0 / CELL, 0.0).astype(BF16)


def fmm_kernel(
    n_seq,
    n_head,
    q_hbm,
    kv_hbm,
    gain_ref,
    att,
    raw,
    q_buf,
    k_buf,
    v_buf,
    k1,
    v1,
    k23,
    v23,
    tok_recv,
    cells_send,
    cells_recv,
    pair,
    cube_recv,
    third_send,
    third,
    near_out,
    near_top,
    own_sum,
    sums,
    splitter,
    q_sem,
    kv_sem,
    tok_ssem,
    tok_rsem,
    cells_ssem,
    cells_rsem,
    pair_ssem,
    pair_rsem,
    cube_ssem,
    cube_rsem,
    third_ssem,
    third_rsem,
    sum_ssem,
    sum_rsem,
):
    seqs, toks, _ = q_hbm.shape
    blocks = toks // BLK
    cells = toks // CELL
    cubes = n_seq // 2
    seq_len = n_seq * toks
    me = lax.axis_index("seq")
    head = lax.axis_index("head")
    core = me % 2
    chip = me // 2
    dev_start = me * toks
    parts = ((0, blocks - 2), (blocks - 2, 2))
    first_half = me < n_seq // 2
    early = jnp.where(first_half & (chip % 2 == 0), EARLY, 0)
    two_pass = jnp.where(first_half, *TWO_PASS)
    has_low = me > 0
    has_high = me < n_seq - 1

    for s in range(seqs):
        pltpu.make_async_copy(kv_hbm.at[s], raw.at[s], kv_sem.at[s]).start()

    barrier = pltpu.get_barrier_semaphore()

    def greet(seq_id, head_id):
        pl.semaphore_signal(
            barrier, inc=1, device_id=(seq_id, head_id), device_id_type=MESH
        )

    greet(me + 1 - 2 * core, head)
    for k in range(1, cubes):
        greet((chip + k) % cubes * 2 + core, head)
    for k in range(1, n_head):
        greet(me, (head + k) % n_head)
    outer = me - 1 + 2 * core
    outer_there = (outer >= 0) & (outer < n_seq)

    @pl.when(outer_there)
    def _():
        greet(outer, head)

    splitter[...] = split_matrix()
    v_buf[:, :, HD:] = jnp.ones((seqs, toks + BLK, HD), BF16)
    spare = 16 - (cubes - 1)
    third[(cubes - 1) * 8 :, :] = jnp.zeros((spare * 8, HD), F32)
    k23[...] = jnp.zeros_like(k23)
    v23[...] = jnp.zeros_like(v23)

    @pl.when(jnp.logical_not(has_low))
    def _():
        k_buf[:, :MARGIN, :] = jnp.zeros((seqs, MARGIN, HD), BF16)
        v_buf[:, :MARGIN, :HD] = jnp.zeros((seqs, MARGIN, HD), BF16)
        k1[:, :32, :] = jnp.zeros((seqs, 32, HD), F32)
        v1[:, :32, :] = jnp.zeros((seqs, 32, HD), F32)

    @pl.when(jnp.logical_not(has_high))
    def _():
        k_buf[:, MARGIN + toks :, :] = jnp.zeros((seqs, MARGIN, HD), BF16)
        v_buf[:, MARGIN + toks :, :HD] = jnp.zeros((seqs, MARGIN, HD), BF16)
        k1[:, 32 + cells :, :] = jnp.zeros((seqs, 32, HD), F32)
        v1[:, 32 + cells :, :] = jnp.zeros((seqs, 32, HD), F32)


    def token_copy(side):
        rows = pl.ds(0, BLK) if side == 0 else pl.ds(2 * toks - BLK, BLK)
        return pltpu.make_async_remote_copy(
            src_ref=kv_hbm.at[:, rows, :],
            dst_ref=tok_recv.at[1 - side],
            send_sem=tok_ssem.at[side],
            recv_sem=tok_rsem.at[1 - side],
            device_id=(me - 1 if side == 0 else me + 1, head),
            device_id_type=MESH,
        )

    def cells_copy(side):
        return pltpu.make_async_remote_copy(
            src_ref=cells_send.at[side],
            dst_ref=cells_recv.at[1 - side],
            send_sem=cells_ssem.at[side],
            recv_sem=cells_rsem.at[1 - side],
            device_id=(me - 1 if side == 0 else me + 1, head),
            device_id_type=MESH,
        )

    there = (has_low, has_high)
    pooler = pool_matrix()
    for s in range(seqs):
        pltpu.make_async_copy(kv_hbm.at[s], raw.at[s], kv_sem.at[s]).wait()

        def pool_chunk(j, carry, s=s):
            start = pl.multiple_of(j * BLK, BLK)
            cell = dot_nn(pooler, raw[s, pl.ds(start, BLK), :])
            at = pl.multiple_of(j * 8 + 32, 8)
            k1[s, pl.ds(at, 8), :] = cell[:8].astype(BF16).astype(F32)
            v1[s, pl.ds(at, 8), :] = cell[8:].astype(BF16).astype(F32)
            return carry

        lax.fori_loop(0, 2 * toks // BLK, pool_chunk, 0, unroll=16)

    for s in range(seqs):
        pltpu.make_async_copy(q_hbm.at[s], q_buf.at[s], q_sem.at[s]).start()

    def split_chunks(sources, places):
        parts = dot_nn(splitter[...], jnp.concatenate(sources, axis=1))
        for i, (s, dst) in enumerate(places):
            mine = parts[:, i * HD : i * HD + HD].astype(BF16)
            k_buf[s, pl.ds(dst, MARGIN), :] = mine[:MARGIN]
            v_buf[s, pl.ds(dst, MARGIN), :HD] = mine[MARGIN:]

    def loop_split(i, carry):
        for s in range(seqs):
            start = pl.multiple_of(i * 2 * BLK, 2 * BLK)
            dst = pl.multiple_of(i * BLK + MARGIN, MARGIN)
            split_chunks(
                [raw[s, pl.ds(start, BLK), :], raw[s, pl.ds(start + BLK, BLK), :]],
                [(s, dst), (s, dst + MARGIN)],
            )
        return carry

    split_steps = toks // BLK
    split_first = jnp.where(first_half, split_steps, 0)

    pool_row = iota((CELL, 2 * cells), 0)
    pool_col = iota((CELL, 2 * cells), 1)
    pool_two = jnp.where(pool_col // CELL == pool_row, 1.0 / CELL, 0.0).astype(BF16)
    for s in range(seqs):
        ones_kv = jnp.concatenate(
            [k1[s, 32 : 32 + cells, :], v1[s, 32 : 32 + cells, :]], axis=0
        ).astype(BF16)
        pair[core, s] = dot_nn(pool_two, ones_kv).astype(BF16)
    pair_copy = pltpu.make_async_remote_copy(
        src_ref=pair.at[core],
        dst_ref=pair.at[core],
        send_sem=pair_ssem,
        recv_sem=pair_rsem,
        device_id=(me + 1 - 2 * core, head),
        device_id_type=MESH,
    )
    for side in range(2):
        at = 32 if side == 0 else cells
        for s in range(seqs):
            cells_send[side, s, :32, :] = k1[s, at : at + 32, :].astype(BF16)
            cells_send[side, s, 32:, :] = v1[s, at : at + 32, :].astype(BF16)

    def cube_copy(slot):
        target = chip + 2 - core - slot
        return pltpu.make_async_remote_copy(
            src_ref=pair,
            dst_ref=cube_recv.at[slot],
            send_sem=cube_ssem.at[slot],
            recv_sem=cube_rsem.at[slot],
            device_id=(target * 2 + core, head),
            device_id_type=MESH,
        )

    def cube_goes(slot):
        target = chip + 2 - core - slot
        return (target >= 0) & (target < cubes) & (slot != 2 - core)

    def cube_comes(slot):
        source = chip - 2 + core + slot
        return (source >= 0) & (source < cubes) & (slot != 2 - core)

    def third_copy(k):
        return pltpu.make_async_remote_copy(
            src_ref=third_send,
            dst_ref=third.at[pl.ds((cubes - 1 - k) * 8, 8), :],
            send_sem=third_ssem.at[k],
            recv_sem=third_rsem.at[cubes - 1 - k],
            device_id=((chip + k) % cubes * 2 + core, head),
            device_id_type=MESH,
        )

    lane = iota((1, EXTRA), 1)
    ones_tile = jnp.ones((EXTRA, HD), BF16)
    eye = iota((HD, HD), 0) == iota((HD, HD), 1)

    def extra_bias(b):
        start = dev_start + b * BLK
        first_lo = start - 2 * BLK
        first_hi = start + 3 * BLK
        second_lo = (first_lo + CUBE) // CUBE * CUBE - 2 * CUBE
        second_hi = (first_hi + CUBE - 1) // CUBE * CUBE + CUBE
        one_pos = jnp.where(
            lane < LOW, first_lo + lane * CELL, start + 384 + (lane - LOW) * CELL
        )
        two_pos = ((chip - 2 + core) * 16 + lane - 2 * LOW) * BLK
        third_slot = lane - 112
        third_cube = (chip + 1 + third_slot) % cubes
        three_pos = third_cube * CUBE
        one_ok = (one_pos >= 0) & (one_pos < seq_len)
        two_ok = (
            (two_pos >= 0)
            & (two_pos < seq_len)
            & (two_pos >= second_lo)
            & (two_pos < second_hi)
            & ((two_pos < first_lo) | (two_pos >= first_hi))
        )
        three_ok = (third_slot < cubes - 1) & (
            (three_pos < second_lo) | (three_pos >= second_hi)
        )
        return jnp.where(
            lane < 2 * LOW,
            jnp.where(one_ok, LEVEL_STEP, NEG),
            jnp.where(
                lane < 112,
                jnp.where(two_ok, 2 * LEVEL_STEP, NEG),
                jnp.where(three_ok, 3 * LEVEL_STEP, NEG),
            ),
        )

    def near_scores(s, b):
        at = pl.multiple_of(b * BLK, BLK)
        return dot_nt(q_buf[s, pl.ds(at, BLK), :], k_buf[s, pl.ds(at, NEAR), :])

    def extra_scores(s, b, bias):
        at = pl.multiple_of(b * BLK, BLK)
        return dot_nt(q_buf[s, pl.ds(at, BLK), :], extras(k1, k23, s, b)) + bias

    def near_values(s, b):
        return v_buf[s, pl.ds(pl.multiple_of(b * BLK, BLK), NEAR), :]

    def extra_values(s, b):
        return jnp.concatenate([extras(v1, v23, s, b), ones_tile], axis=1)

    def weigh(score, top):
        return jnp.exp2((score - top) * EXP_SCALE).astype(BF16)

    def extras(one, rest, s, b):
        cell_at = pl.multiple_of(b * CELL, CELL)
        return jnp.concatenate(
            [
                one[s, pl.ds(cell_at, LOW), :],
                one[s, pl.ds(pl.multiple_of(cell_at + 56, 8), LOW), :],
                rest[s],
            ],
            axis=0,
        ).astype(BF16)

    def items_of(places):
        return [(s, block_at(place), place) for place in places for s in range(seqs)]

    def near_part(items):
        scores = [near_scores(s, b) for s, b, _ in items]
        tops = [jnp.max(score, axis=1, keepdims=True) for score in scores]
        for (s, b, place), score, top in zip(items, scores, tops):
            near_out[place, s] = dot_nn(weigh(score, top), near_values(s, b))
            near_top[place, s] = jnp.broadcast_to(top, (BLK, HD))

    def finish(s, b, place, summed, row_total):
        at = pl.multiple_of(b * BLK, BLK)
        result = (summed / row_total).astype(BF16)
        att[s, pl.ds(at, BLK), :] = result
        wide = result.astype(F32)
        square = jnp.sum(wide * wide, axis=1, keepdims=True)
        for half in range(2):
            picked = jnp.where(eye, square[half * HD : half * HD + HD], 0.0)
            row = 2 * s + half
            own_sum[place, row : row + 1, :] = jnp.sum(picked, axis=0, keepdims=True)

    def merge(items, scores, values):
        tops = [
            jnp.maximum(near_top[slot, s], jnp.max(score, axis=1, keepdims=True))
            for (s, _, _, slot), score in zip(items, scores)
        ]
        parts = [
            dot_nn(weigh(score, top), values(s, b))
            for (s, b, _, _), score, top in zip(items, scores, tops)
        ]
        for (s, b, place, slot), part, top in zip(items, parts, tops):
            shrink = jnp.exp2((near_top[slot, s] - top) * EXP_SCALE)
            summed = near_out[slot, s, :, :HD] * shrink + part[:, :HD]
            row_total = near_out[slot, s, :, HD:] * shrink + part[:, HD:]
            finish(s, b, place, summed, row_total)

    def far_part(items):
        scores = [extra_scores(s, b, extra_bias(b)) for s, b, _ in items]
        merge([(s, b, place, place) for s, b, place in items], scores, extra_values)

    def halo_at(b):
        return pl.multiple_of(jnp.where(b == 0, 0, MARGIN + toks), MARGIN)

    def edge_local(items):
        span = NEAR - MARGIN
        near = []
        for s, b, _ in items:
            at = pl.multiple_of(b * BLK, BLK)
            local = pl.multiple_of(at + jnp.where(b == 0, MARGIN, 0), MARGIN)
            keys = k_buf[s, pl.ds(local, span), :]
            near.append(dot_nt(q_buf[s, pl.ds(at, BLK), :], keys))
        far = [extra_scores(s, b, extra_bias(b)) for s, b, _ in items]
        tops = [
            jnp.maximum(
                jnp.max(x, axis=1, keepdims=True), jnp.max(y, axis=1, keepdims=True)
            )
            for x, y in zip(near, far)
        ]
        for (s, b, place), x, y, top in zip(items, near, far, tops):
            at = b * BLK + jnp.where(b == 0, MARGIN, 0)
            values = v_buf[s, pl.ds(pl.multiple_of(at, MARGIN), span), :]
            slot = place - (blocks - 2)
            near_out[slot, s] = dot_nn(weigh(x, top), values) + dot_nn(
                weigh(y, top), extra_values(s, b)
            )
            near_top[slot, s] = jnp.broadcast_to(top, (BLK, HD))

    def halo_scores(s, b):
        at = pl.multiple_of(b * BLK, BLK)
        pos = dev_start + halo_at(b) - MARGIN + iota((1, MARGIN), 1)
        bias = jnp.where((pos >= 0) & (pos < seq_len), 0.0, NEG)
        keys = k_buf[s, pl.ds(halo_at(b), MARGIN), :]
        return dot_nt(q_buf[s, pl.ds(at, BLK), :], keys) + bias

    def halo_values(s, b):
        return v_buf[s, pl.ds(halo_at(b), MARGIN), :]

    def edge_halo(items):
        scores = [halo_scores(s, b) for s, b, _ in items]
        with_slots = [(s, b, place, place - (blocks - 2)) for s, b, place in items]
        merge(with_slots, scores, halo_values)

    def whole_part(items):
        near = [near_scores(s, b) for s, b, _ in items]
        far = [extra_scores(s, b, extra_bias(b)) for s, b, _ in items]
        tops = [
            jnp.maximum(
                jnp.max(x, axis=1, keepdims=True), jnp.max(y, axis=1, keepdims=True)
            )
            for x, y in zip(near, far)
        ]
        outs = [
            dot_nn(weigh(x, top), near_values(s, b))
            + dot_nn(weigh(y, top), extra_values(s, b))
            for (s, b, _), x, y, top in zip(items, near, far, tops)
        ]
        for (s, b, place), out in zip(items, outs):
            finish(s, b, place, out[:, :HD], out[:, HD:])

    def sum_copy(part, k):
        places = pl.ds(*parts[part])
        return pltpu.make_async_remote_copy(
            src_ref=own_sum.at[places],
            dst_ref=sums.at[n_head - 1 - k, places],
            send_sem=sum_ssem.at[part, k],
            recv_sem=sum_rsem.at[part, n_head - 1 - k],
            device_id=(me, (head + k) % n_head),
            device_id_type=MESH,
        )

    def block_at(place):
        inner_end = blocks - 4
        return jnp.where(
            place < inner_end,
            place + 2,
            jnp.where(
                place < inner_end + 2,
                1 + (place - inner_end) * (blocks - 3),
                (place - inner_end - 2) * (blocks - 1),
            ),
        )

    def normalize(place, carry):
        b = block_at(place)
        acc = own_sum[place]
        for k in range(n_head - 1):
            acc = acc + sums[k, place]
        scale = 1.0 / jnp.sqrt(acc / (HD * n_head) + 1e-06)
        gain = gain_ref[...]
        for s in range(seqs):
            for half in range(2):
                at = pl.multiple_of(b * BLK + half * HD, HD)
                row = 2 * s + half
                picked = jnp.where(eye, scale[row : row + 1], 0.0)
                column = jnp.sum(picked, axis=1, keepdims=True)
                wide = att[s, pl.ds(at, HD), :].astype(F32)
                att[s, pl.ds(at, HD), :] = (wide * column * gain).astype(BF16)
        return carry

    def loop_near(i, carry):
        near_part(items_of((2 * i, 2 * i + 1)))
        return carry

    def loop_far(i, carry):
        far_part(items_of((2 * i, 2 * i + 1)))
        return carry

    def loop_whole(i, carry):
        whole_part(items_of((2 * i, 2 * i + 1)))
        return carry

    def loop_local(i, carry):
        edge_local(items_of((2 * i, 2 * i + 1)))
        return carry

    def loop_edge(i, carry):
        edge_halo(items_of((2 * i, 2 * i + 1)))
        return carry

    def q_wait():
        for s in range(seqs):
            pltpu.make_async_copy(q_hbm.at[s], q_buf.at[s], q_sem.at[s]).wait()

    lax.fori_loop(0, split_first, loop_split, 0)

    @pl.when(first_half)
    def _():
        q_wait()

    lax.fori_loop(0, early, loop_near, 0)
    pl.semaphore_wait(barrier, cubes + n_head - 1 + outer_there.astype(jnp.int32))
    pair_copy.start()
    split_then = jnp.where(first_half, split_steps, SPLIT_THEN)
    lax.fori_loop(split_first, split_then, loop_split, 0)
    pair_copy.wait()
    for s in range(seqs):
        both = pair[0, s].astype(F32) + pair[1, s].astype(F32)
        for half in range(2):
            mean = jnp.sum(both[8 * half : 8 * half + 8], axis=0, keepdims=True) / CELL
            third_send[2 * s + half : 2 * s + half + 1, :] = mean.astype(BF16).astype(F32)

    for k in range(1, cubes):
        third_copy(k).start()
    for slot in range(4):

        @pl.when(cube_goes(slot))
        def _(slot=slot):
            cube_copy(slot).start()

    for side in range(2):

        @pl.when(there[side])
        def _(side=side):
            cells_copy(side).start()
            token_copy(side).start()

    lax.fori_loop(split_then, split_steps, loop_split, 0)

    @pl.when(jnp.logical_not(first_half))
    def _():
        q_wait()

    lax.fori_loop(early, two_pass, loop_near, 0)

    for side in range(2):

        @pl.when(there[side])
        def _(side=side):
            cells_copy(1 - side).wait_recv()
            at = 0 if side == 0 else 32 + cells
            for s in range(seqs):
                k1[s, at : at + 32, :] = cells_recv[side, s, :32, :].astype(F32)
                v1[s, at : at + 32, :] = cells_recv[side, s, 32:, :].astype(F32)

    for k in range(1, cubes):
        third_copy(k).wait_recv()
    for s in range(seqs):
        k23[s, 64:, :] = third[pl.ds(2 * s, 16, stride=8), :]
        v23[s, 64:, :] = third[pl.ds(2 * s + 1, 16, stride=8), :]
    for slot in range(4):
        for half in range(2):
            at = slot * 16 + half * 8

            @pl.when(slot == 2 - core)
            def _(half=half, at=at):
                for s in range(seqs):
                    tile = pair[half, s].astype(F32)
                    k23[s, at : at + 8, :] = tile[:8]
                    v23[s, at : at + 8, :] = tile[8:]

            @pl.when(cube_comes(slot))
            def _(slot=slot, half=half, at=at):
                if half == 0:
                    cube_copy(slot).wait_recv()
                for s in range(seqs):
                    tile = cube_recv[slot, half, s].astype(F32)
                    k23[s, at : at + 8, :] = tile[:8]
                    v23[s, at : at + 8, :] = tile[8:]

    lax.fori_loop(0, two_pass, loop_far, 0)
    lax.fori_loop(two_pass, blocks // 2 - 1, loop_whole, 0)
    for k in range(1, n_head):
        sum_copy(0, k).start()

    lax.fori_loop(blocks // 2 - 1, blocks // 2, loop_local, 0)
    for side in range(2):

        @pl.when(there[side])
        def _(side=side):
            token_copy(1 - side).wait_recv()
            at = 0 if side == 0 else MARGIN + toks
            for s in range(0, seqs, 2):
                pair_of = range(s, min(s + 2, seqs))
                split_chunks(
                    [tok_recv[side, i] for i in pair_of], [(i, at) for i in pair_of]
                )

    lax.fori_loop(blocks // 2 - 1, blocks // 2, loop_edge, 0)
    for k in range(1, n_head):
        sum_copy(1, k).start()
    for k in range(1, n_head):
        sum_copy(0, k).wait_recv()
    lax.fori_loop(0, blocks - 2, normalize, 0)
    for k in range(1, n_head):
        sum_copy(1, k).wait_recv()
    lax.fori_loop(blocks - 2, blocks, normalize, 0)

    for part in range(2):
        for k in range(1, n_head):
            sum_copy(part, k).wait_send()
    for side in range(2):

        @pl.when(there[side])
        def _(side=side):
            token_copy(side).wait_send()
            cells_copy(side).wait_send()

    for slot in range(4):

        @pl.when(cube_goes(slot))
        def _(slot=slot):
            cube_copy(slot).wait_send()

    for k in range(1, cubes):
        third_copy(k).wait_send()


def attention(queries, pairs, gain, n_seq, n_head):
    seqs, toks, _ = queries.shape
    blocks = toks // BLK
    cells = toks // CELL
    cubes = n_seq // 2
    assert toks == CUBE // 2 and cubes <= 16 and 2 * seqs <= 8
    vmem = pltpu.VMEM
    dma = pltpu.SemaphoreType.DMA
    hbm = pl.BlockSpec(memory_space=pl.ANY)
    return pl.pallas_call(
        functools.partial(fmm_kernel, n_seq, n_head),
        out_shape=vmem((seqs, toks, HD), BF16),
        in_specs=[hbm, hbm, pl.BlockSpec(memory_space=vmem)],
        out_specs=pl.BlockSpec(memory_space=vmem),
        scratch_shapes=[
            vmem((seqs, 2 * toks, HD), BF16),
            vmem((seqs, toks, HD), BF16),
            vmem((seqs, toks + BLK, HD), BF16),
            vmem((seqs, toks + BLK, 2 * HD), BF16),
            vmem((seqs, cells + 64, HD), F32),
            vmem((seqs, cells + 64, HD), F32),
            vmem((seqs, 80, HD), F32),
            vmem((seqs, 80, HD), F32),
            vmem((2, seqs, BLK, HD), BF16),
            vmem((2, seqs, 64, HD), BF16),
            vmem((2, seqs, 64, HD), BF16),
            vmem((2, seqs, CELL, HD), BF16),
            vmem((4, 2, seqs, CELL, HD), BF16),
            vmem((8, HD), F32),
            vmem((16 * 8, HD), F32),
            vmem((2 * max(TWO_PASS), seqs, BLK, 2 * HD), F32),
            vmem((2 * max(TWO_PASS), seqs, BLK, HD), F32),
            vmem((blocks, 8, HD), F32),
            vmem((n_head - 1, blocks, 8, HD), F32),
            vmem((BLK, BLK), BF16),
            dma((seqs,)),
            dma((seqs,)),
            dma((2,)),
            dma((2,)),
            dma((2,)),
            dma((2,)),
            dma(()),
            dma(()),
            dma((4,)),
            dma((4,)),
            dma((16,)),
            dma((16,)),
            dma((2, n_head)),
            dma((2, n_head)),
        ],
        compiler_params=pltpu.CompilerParams(
            collective_id=0, has_side_effects=True, vmem_limit_bytes=61 * 2**20
        ),
        cost_estimate=pl.CostEstimate(
            flops=4 * seqs * toks * 640 * HD,
            bytes_accessed=8 * seqs * toks * HD,
            transcendentals=seqs * toks * 640,
        ),
    )(queries, pairs, gain)


def on_device(n_seq, n_head, queries, keys_values, norm_gain):
    seqs, toks, width = queries.shape
    pairs = keys_values.reshape(seqs, 2 * toks, width)
    return attention(queries, pairs, norm_gain.reshape(1, HD), n_seq, n_head)


def solution(mesh):
    n_seq, n_head = mesh.shape["seq"], mesh.shape["head"]
    in_specs = (P(None, "seq", "head"), P(None, "seq", None, "head"), P("head"))
    return jax.shard_map(
        functools.partial(on_device, n_seq, n_head),
        mesh=mesh,
        in_specs=in_specs,
        out_specs=P(None, "seq", "head"),
        check_vma=False,
    )
```
